128 devices in a mesh: scen: 16 (over x, y), col: 8 (over z, core).
Axes of the slice: x: 4, y: 4, z: 4, core: 2. Of those that a mesh axis runs over, the one named last changes fastest.
Arguments:
- border: bfloat16 [64, 256, 2048], P('scen', None, 'col'), may hold values from -0.24077223 to 0.24077223
- touched: int32 [64, 8], replicated, may hold values from 0 to 63, as said below
- barrier: float32 [16384], replicated, may hold values from 0.5 to 8
Outputs:
- factored: float32 [16384, 16384], P('scen', 'col')
The draws below stay inside these ranges and needn't reach their ends.
Inputs may be any that keep to these rules, and one draw needn't show every extreme that they name: Column blocks fall into 8 classes by their remainder modulo 8: touched[s, k] % 8 == k, so each scenario touches one block of each class.
All inputs are finite; a program needn't handle non-finite values.
Results may differ from the reference program's by a relative error of at most 0.0013.
Values may be sent and summed in bfloat16 or wider, within the bound.
A program may use at most 192 MiB of HBM per device.

```python
import math
import jax
import jax.numpy as jnp
from jax import lax

N = 16384
TB = 256
KT = 8
BROWS = 256
PW = 1024
SCEN = 64
N_SCEN = 16
N_COL = 8


def draw_touched(key, part):
    key = jax.random.fold_in(key, 11)
    levels = jax.random.randint(key, (SCEN, KT), 0, N // (TB * KT), dtype=jnp.int32)
    levels = levels.at[0].set(N // (TB * KT) - 1)
    levels = levels.at[1].set(0)
    return (jnp.arange(KT, dtype=jnp.int32)[None, :] + KT * levels).astype(jnp.int32)


def draw_border(key, part):
    key = jax.random.fold_in(key, 7)
    own_key = jax.random.fold_in(key, 1)
    row_key = jax.random.fold_in(key, 2)
    spread = float(SCEN * KT * BROWS * TB // N) ** (-0.5)
    common = 0.8 * float(BROWS) ** (-0.5)
    single = jnp.clip(jax.random.normal(own_key, (SCEN, BROWS, KT * TB), jnp.float32), -4.0, 4.0) * spread
    shared = jnp.clip(jax.random.normal(row_key, (SCEN, BROWS, 1), jnp.float32), -3.0, 3.0) * common
    return (single + shared).astype(jnp.bfloat16)


def setup_inputs(seed: int = 0) -> dict:
    arg_keys = jax.random.split(jax.random.key(seed), 4)
    border = draw_border(jax.random.fold_in(arg_keys[3], 71), 0)
    touched = draw_touched(jax.random.fold_in(arg_keys[3], 71), 0)
    barrier = jnp.clip(jnp.exp(jax.random.uniform(arg_keys[2], (N,), jnp.float32, math.log(0.5), math.log(8.0))), 0.5, 8.0)
    return {"border": border, "touched": touched, "barrier": barrier}


def reference(border, touched, barrier):
    schur_full = jnp.diag(barrier)
    offsets = jnp.arange(TB, dtype=jnp.int32)

    def add_scenario(scenario, running):
        columns = (touched[scenario][:, None] * TB + offsets[None, :]).reshape(-1).astype(jnp.int32)
        border_block = border[scenario]
        gram_block = jnp.dot(border_block.T.astype(jnp.float32), border_block.astype(jnp.float32), preferred_element_type=jnp.float32)
        return running.at[columns[:, None], columns[None, :]].add(gram_block)
    schur_full = lax.fori_loop(0, SCEN, add_scenario, schur_full)
    corner = jnp.linalg.cholesky(schur_full[:PW, :PW])
    solved_panel = lax.linalg.triangular_solve(corner, schur_full[:, :PW], left_side=False, lower=True, transpose_a=True)
    lower_panel = solved_panel[PW:]
    lower_right = schur_full[PW:, PW:] - jnp.dot(lower_panel, lower_panel.T, precision=lax.Precision.HIGHEST)
    upper_band = jnp.concatenate([solved_panel[:PW], schur_full[:PW, PW:]], axis=1)
    bottom = jnp.concatenate([lower_panel, lower_right], axis=1)
    updated = jnp.concatenate([upper_band, bottom], axis=0)
    cyclic = updated.reshape(N // (TB * N_SCEN), N_SCEN, TB, N // (TB * N_COL), N_COL, TB)
    return cyclic.transpose(1, 0, 2, 4, 3, 5).reshape(N, N)
```

```python
import jax
import jax.numpy as jnp
from jax import lax
from jax.experimental import pallas as pl
from jax.experimental.pallas import tpu as pltpu
from jax.sharding import PartitionSpec as P

N = 16384
TB = 256
KT = 8
PW = 1024
SCEN = 64
NB = 128
F32 = jnp.float32
BF16 = jnp.bfloat16
HIGHEST = lax.Precision.HIGHEST
MESH = pl.DeviceIdType.MESH
DMA = pltpu.SemaphoreType.DMA
NT = (((1,), (1,)), ((), ()))
TN = (((0,), (0,)), ((), ()))
MIB = 1024 * 1024

COMBOS = [
    (0, 0), (1, 0), (3, 0), (0, 1), (0, 3), (2, 0), (0, 2), (1, 1),
    (1, 3), (3, 1), (3, 3), (2, 1), (2, 3), (1, 2), (3, 2), (2, 2),
]


def plane_slots():
    slots = {}
    for e1, e2 in COMBOS:
        if e2 == 0:
            kinds = {0: (0, 1, 2, 3), 1: (0, 2, 3)}.get(e1, (2, 3))
        else:
            kinds = (2,) if e2 == 1 else ()
        for kind in kinds:
            slots[(e1, e2, kind)] = len(slots)
    return slots


SLOTS = plane_slots()


def rem4(v):
    return lax.rem(v + 8, 4)


def place():
    p = lax.axis_index("scen")
    q = lax.axis_index("col")
    return p, q, p // 4, lax.rem(p, 4), q // 2, lax.rem(q, 2)


def dev(x, y, z, c):
    return (x * 4 + y, z * 2 + c)


def remote(src, dst, send, recv, device):
    return pltpu.make_async_remote_copy(
        src_ref=src, dst_ref=dst, send_sem=send, recv_sem=recv,
        device_id=device, device_id_type=MESH,
    )


def greet(devices):
    bar = pltpu.get_barrier_semaphore()
    for d in devices:
        pl.semaphore_signal(bar, inc=1, device_id=d, device_id_type=MESH)
    pl.semaphore_wait(bar, len(devices))


def lane(v):
    return pl.multiple_of(v, 128)


class Plane:
    def __init__(self, own, tiles, send_sem, recv_sem):
        self.own, self.tiles = own, tiles
        self.send_sem, self.recv_sem = send_sem, recv_sem
        self.p, self.q, self.x, self.y, self.z, self.c = place()

    def geom(self, j):
        sy = j // 2
        return 1 - sy, sy, 1 - 2 * lax.rem(j, 2)

    def tile(self, e1, e2, j):
        sx, sy, d = self.geom(j)
        ox = rem4(self.x - d * (e1 * sx + e2 * sy))
        oy = rem4(self.y - d * (e1 * sy + e2 * sx))
        return 4 * (ox * 4 + oy) + j

    def event(self, e1, e2, extra=None):
        def body(j, _):
            sx, sy, d = self.geom(j)
            s = self.tile(e1, e2, j)
            dst = self.tiles(s)
            if (e1, e2) == (0, 0):
                src = self.own(j)
            else:
                src = dst
                remote(
                    src, src, self.send_sem.at[0],
                    self.recv_sem.at[(e1 * 4 + e2) * 4 + j], (self.p, self.q),
                ).wait_recv()

            def send(kind, first, sign, r1, r2):
                dx = (sx if first else sy) * d * sign
                dy = (sy if first else sx) * d * sign
                remote(
                    src, dst, self.send_sem.at[SLOTS[(e1, e2, kind)] * 4 + j],
                    self.recv_sem.at[(r1 * 4 + r2) * 4 + j],
                    dev(rem4(self.x + dx), rem4(self.y + dy), self.z, self.c),
                ).start()

            if e2 == 0:
                if e1 == 0:
                    send(0, True, 1, 1, 0)
                    send(1, True, -1, 3, 0)
                if e1 == 1:
                    send(0, True, 1, 2, 0)
                send(2, False, 1, e1, 1)
                send(3, False, -1, e1, 3)
            elif e2 == 1:
                send(2, False, 1, e1, 2)
            if extra is not None:
                extra(src, s, (e1 * 4 + e2) * 4 + j, d)
            return 0

        lax.fori_loop(0, 4, body, 0)

    def drain(self):
        t = self.tiles(0)

        def body(i, _):
            remote(t, t, self.send_sem.at[i], self.recv_sem.at[0], (self.p, self.q)).wait_send()
            return 0

        lax.fori_loop(0, 4 * len(SLOTS), body, 0)


def plane_peers():
    p, q, x, y, z, c = place()
    return [
        dev(rem4(x + 1), y, z, c), dev(rem4(x - 1), y, z, c),
        dev(x, rem4(y + 1), z, c), dev(x, rem4(y - 1), z, c),
    ]


def gather_kernel(b_ref, g_ref, h_ref, loc, ssem, rsem, zsem, psem, hsem):
    p, q, x, y, z, c = place()
    k = lax.rem(p, 8)
    zs, cs = k // 2, lax.rem(k, 2)
    here, partner = (p, q), dev(x, y, z, 1 - c)
    greet(plane_peers() + [dev(x, y, rem4(z + 1), c), dev(x, y, rem4(z - 1), c), partner])
    own = pltpu.make_async_copy(b_ref, g_ref.at[pl.ds(4 * p, 4)], loc)
    own.start()
    chain = c == cs
    source = jnp.logical_and(chain, z == zs)
    plane = Plane(lambda j: b_ref.at[j], lambda s: g_ref.at[s], ssem, rsem)

    def feed(src, s, h, d):
        @pl.when(source)
        def _():
            remote(src, h_ref.at[s], zsem.at[h], hsem.at[h], dev(x, y, rem4(z + d), c)).start()
            remote(src, h_ref.at[s], psem.at[h], hsem.at[h], partner).start()

    def relay(e1, e2, r):
        def body(j, _):
            d = 1 - 2 * lax.rem(j, 2)
            h = (e1 * 4 + e2) * 4 + j

            @pl.when(jnp.logical_and(chain, rem4((z - zs) * d) == r))
            def _():
                t = h_ref.at[plane.tile(e1, e2, j)]
                remote(t, t, zsem.at[0], hsem.at[h], here).wait_recv()
                if r < 3:
                    remote(t, t, zsem.at[h], hsem.at[h], dev(x, y, rem4(z + d), c)).start()
                remote(t, t, psem.at[h], hsem.at[h], partner).start()

            return 0

        lax.fori_loop(0, 4, body, 0)

    for n in range(len(COMBOS) + 3):
        if n < len(COMBOS):
            plane.event(*COMBOS[n], extra=feed)
        for r in (1, 2, 3):
            if 0 <= n - r < len(COMBOS):
                relay(*COMBOS[n - r], r)
    own.wait()
    plane.drain()
    t = g_ref.at[0]

    def last(i, _):
        d = 1 - 2 * lax.rem(i, 2)

        @pl.when(jnp.logical_and(chain, rem4((z - zs) * d) < 3))
        def _():
            remote(t, t, zsem.at[i], hsem.at[0], here).wait_send()

        @pl.when(chain)
        def _():
            remote(t, t, psem.at[i], hsem.at[0], here).wait_send()

        @pl.when(jnp.logical_not(chain))
        def _():
            remote(t, t, zsem.at[0], hsem.at[i], here).wait_recv()

        return 0

    lax.fori_loop(0, SCEN, last, 0)


def gather_borders(border):
    tiles = jax.ShapeDtypeStruct((SCEN, TB, TB), BF16)
    hbm = pl.BlockSpec(memory_space=pl.ANY)
    return pl.pallas_call(
        gather_kernel,
        out_shape=(tiles, tiles),
        in_specs=[hbm],
        out_specs=(hbm, hbm),
        scratch_shapes=[DMA(()), DMA((60,)), DMA((64,)), DMA((64,)), DMA((64,)), DMA((64,))],
        compiler_params=pltpu.CompilerParams(collective_id=0, has_side_effects=True),
        name="gather_borders",
    )(border)


PER_STEP = 4


def schur_kernel(touched_ref, g_ref, h_ref, bar_ref, out_ref):
    p, q = lax.axis_index("scen"), lax.axis_index("col")
    k = lax.rem(p, 8)
    step = pl.program_id(0)
    diagonal = k == q

    @pl.when(step == 0)
    def _():
        out_ref[...] = jnp.zeros_like(out_ref)

        @pl.when(diagonal)
        def _():
            eye = lax.broadcasted_iota(jnp.int32, (TB, TB), 0) == lax.broadcasted_iota(
                jnp.int32, (TB, TB), 1
            )
            for a in range(4):
                col = lane((2 * a + p // 8) * TB)
                row = bar_ref[pl.ds(a * 16 + p, 1), :]
                out_ref[a * TB:(a + 1) * TB, pl.ds(col, TB)] = jnp.where(eye, row, 0.0)

    for i in range(PER_STEP):
        s = step * PER_STEP + i
        big_row = touched_ref[s * KT + k]

        @pl.when(lax.rem(big_row, 16) == p)
        def _():
            row = pl.multiple_of((big_row // 16) * TB, TB)
            col = lane((touched_ref[s * KT + q] // 8) * TB)
            left = jnp.where(diagonal, g_ref[i], h_ref[i])
            out_ref[pl.ds(row, TB), pl.ds(col, TB)] += lax.dot_general(
                left, g_ref[i], TN, preferred_element_type=F32
            )


def assemble(touched, gathered, rows, barrier):
    block = pl.BlockSpec((PER_STEP, TB, TB), lambda i, t: (i, 0, 0))
    return pl.pallas_call(
        schur_kernel,
        out_shape=jax.ShapeDtypeStruct((1024, 2048), F32),
        grid_spec=pltpu.PrefetchScalarGridSpec(
            num_scalar_prefetch=1,
            grid=(SCEN // PER_STEP,),
            in_specs=[block, block, pl.BlockSpec((N // TB, TB), lambda i, t: (0, 0))],
            out_specs=pl.BlockSpec((1024, 2048), lambda i, t: (0, 0)),
        ),
        compiler_params=pltpu.CompilerParams(vmem_limit_bytes=48 * MIB),
        name="assemble",
    )(touched.reshape(-1), gathered, rows, barrier.reshape(N // TB, TB))


def spread_kernel(s_ref, pk_ref, raw_ref, st_ref, loc, ssend, srecv, zsend, zrecv,
                  xsend, xrecv, csend, crecv, asend, arecv):
    p, q, x, y, z, c = place()
    here, partner = (p, q), dev(x, y, z, 1 - c)
    greet([(lax.rem(p + i, 16), q) for i in range(1, 16)]
          + [(p, lax.rem(q + i, 8)) for i in range(1, 8)])
    holds = q < 4
    corner = jnp.logical_and(holds, jnp.logical_and(p < 4, p >= q))

    def cols(k, m):
        return pl.ds(lane((k * (k + 1) // 2 + m) * TB), TB)

    def scatter(i, wait):
        g = lax.rem(p + i, 16)
        cp = remote(s_ref.at[pl.ds(2 * g, 2), :, pl.ds(0, TB)], st_ref.at[p],
                    ssend.at[i - 1], srecv.at[p], (g, q))
        cp.wait_send() if wait else cp.start()

    own_tile = pltpu.make_async_copy(
        s_ref.at[pl.ds(2 * p, 2), :, pl.ds(0, TB)], st_ref.at[lax.rem(p, 4)], loc.at[0])

    @pl.when(corner)
    def _():
        for i in range(1, 16):
            scatter(i, False)
        own_tile.start()

    def rows_to(i):
        to = lax.rem(q + i, 8)
        return remote(s_ref.at[pl.ds(16 * to, 16), :, pl.ds(0, TB)],
                      raw_ref.at[:, :, pl.ds(lane(lax.rem(q, 4) * TB), TB)],
                      asend.at[i - 1], arecv.at[lax.rem(q, 4)], (p, to))

    own_rows = pltpu.make_async_copy(
        s_ref.at[pl.ds(16 * q, 16), :, pl.ds(0, TB)],
        raw_ref.at[:, :, pl.ds(lane(lax.rem(q, 4) * TB), TB)], loc.at[1])

    @pl.when(holds)
    def _():
        for i in range(1, 8):
            rows_to(i).start()
        own_rows.start()

    def fan(k, i):
        to = lax.rem(q + i, 8)
        half = lax.rem(to, 2)
        m = lax.rem(q, 4)
        return remote(st_ref.at[k, half], pk_ref.at[p, half, :, cols(k, m)],
                      zsend.at[k * 7 + i - 1], zrecv.at[k * 4 + m], (p, to))

    def keep(k):
        return pltpu.make_async_copy(
            st_ref.at[k, c], pk_ref.at[p, c, :, cols(k, lax.rem(q, 4))], loc.at[2 + k])

    for k in range(4):
        @pl.when(q <= k)
        def _():
            @pl.when(p == k)
            def _():
                own_tile.wait()

            @pl.when(p != k)
            def _():
                remote(st_ref.at[k], st_ref.at[k], ssend.at[0], srecv.at[k], here).wait_recv()

            for i in range(1, 8):
                fan(k, i).start()
            keep(k).start()

    for k in range(4):
        for m in range(k + 1):
            @pl.when(q == m)
            def _():
                keep(k).wait()

            @pl.when(q != m)
            def _():
                t = pk_ref.at[p, c, :, cols(k, m)]
                remote(t, t, zsend.at[0], zrecv.at[k * 4 + m], here).wait_recv()

    def shard(i):
        return remote(pk_ref.at[p, c], pk_ref.at[p, c], xsend.at[i - 1], xrecv.at[i - 1],
                      (lax.rem(p + i, 16), q))

    for i in range(1, 16):
        shard(i).start()
    for i in range(1, 16):
        t = pk_ref.at[lax.rem(p + 16 - i, 16), c]
        remote(t, t, xsend.at[i - 1], xrecv.at[i - 1], here).wait_recv()
    swap = remote(pk_ref.at[:, c], pk_ref.at[:, c], csend, crecv, partner)
    swap.start()

    for i in range(1, 16):
        shard(i).wait_send()

    @pl.when(corner)
    def _():
        for i in range(1, 16):
            scatter(i, True)

    @pl.when(holds)
    def _():
        for i in range(1, 8):
            rows_to(i).wait_send()
        own_rows.wait()

    for k in range(4):
        @pl.when(q <= k)
        def _():
            for i in range(1, 8):
                fan(k, i).wait_send()

    for m in range(4):
        @pl.when(q != m)
        def _():
            t = raw_ref.at[:, :, pl.ds(m * TB, TB)]
            remote(t, t, asend.at[0], arecv.at[m], here).wait_recv()

    swap.wait_send()
    t = pk_ref.at[:, 1 - c]
    remote(t, t, csend, crecv, here).wait_recv()


def spread(schur):
    hbm = pl.BlockSpec(memory_space=pl.ANY)
    return pl.pallas_call(
        spread_kernel,
        out_shape=(
            jax.ShapeDtypeStruct((16, 2, 8, 2560), F32),
            jax.ShapeDtypeStruct((16, 8, PW), F32),
        ),
        in_specs=[hbm],
        out_specs=(hbm, hbm),
        scratch_shapes=[
            pltpu.VMEM((4, 2, 8, TB), F32), DMA((6,)), DMA((15,)), DMA((4,)), DMA((28,)),
            DMA((16,)), DMA((15,)), DMA((15,)), DMA(()), DMA(()), DMA((7,)), DMA((4,)),
        ],
        compiler_params=pltpu.CompilerParams(collective_id=1, has_side_effects=True),
        name="spread_corner",
    )(schur.reshape(128, 8, 2048))


def pair_step(a0, b, d, r0, r1, g0, g1):
    det = a0 * d - b * b
    inv = 1.0 / det
    q0 = lax.rsqrt(a0)
    q1 = lax.rsqrt(a0 * det)
    ci, bi, ai = d * inv, b * inv, a0 * inv
    x0, x1 = g0 * q0, (a0 * g1 - b * g0) * q1
    z0, z1 = ci * r0 - bi * r1, ai * r1 - bi * r0
    m0, m1 = ci * g0 - bi * g1, ai * g1 - bi * g0
    return x0, x1, z0, z1, m0, m1, ci, bi, ai


def four_columns(a, m, o):
    c = [jnp.broadcast_to(a[:, o + t:o + t + 1], (NB, NB)) for t in range(4)]
    r = [a[o + t:o + t + 1, :] for t in range(4)]
    g = [m[o + t:o + t + 1, :] for t in range(4)]
    w = [[c[u][o + t:o + t + 1, :] for u in range(t + 1)] for t in range(4)]
    x0, x1, z0, z1, m0, m1, ci, bi, ai = pair_step(
        w[0][0], w[1][0], w[1][1], r[0], r[1], g[0], g[1])
    z02, z12 = ci * w[2][0] - bi * w[2][1], ai * w[2][1] - bi * w[2][0]
    z03, z13 = ci * w[3][0] - bi * w[3][1], ai * w[3][1] - bi * w[3][0]
    w22 = w[2][2] - w[2][0] * z02 - w[2][1] * z12
    w32 = w[3][2] - w[3][0] * z02 - w[3][1] * z12
    w33 = w[3][3] - w[3][0] * z03 - w[3][1] * z13
    r2 = r[2] - w[2][0] * z0 - w[2][1] * z1
    r3 = r[3] - w[3][0] * z0 - w[3][1] * z1
    g2 = g[2] - w[2][0] * m0 - w[2][1] * m1
    g3 = g[3] - w[3][0] * m0 - w[3][1] * m1
    x2, x3, z2, z3, m2, m3, _, _, _ = pair_step(w22, w32, w33, r2, r3, g2, g3)
    zt0, zt1 = z0 - z02 * z2 - z03 * z3, z1 - z12 * z2 - z13 * z3
    mt0, mt1 = m0 - z02 * m2 - z03 * m3, m1 - z12 * m2 - z13 * m3
    a = a - c[0] * zt0 - c[1] * zt1 - (c[2] * z2 + c[3] * z3)
    m = m - c[0] * mt0 - c[1] * mt1 - (c[2] * m2 + c[3] * m3)
    return a, m, [x0, x1, x2, x3]


def invert_factor(a, out_ref):
    eye = (
        lax.broadcasted_iota(jnp.int32, (NB, NB), 0)
        == lax.broadcasted_iota(jnp.int32, (NB, NB), 1)
    ).astype(F32)

    def body(it, carry):
        a, m = carry
        rows = []
        for o in range(0, 16, 4):
            a, m, x = four_columns(a, m, o)
            rows += x
        out_ref[pl.ds(pl.multiple_of(it * 16, 16), 16), :] = jnp.concatenate(rows, 0)
        a = pltpu.roll(a, NB - 16, 1)
        return jnp.concatenate([a[16:], a[:16]], 0), jnp.concatenate([m[16:], m[:16]], 0)

    lax.fori_loop(0, NB // 16, body, (a, eye))


def factor_kernel(pk_ref, raw_ref, pf_ref, pb_ref, a_ref, x_ref):
    end = PW + NB
    for k in range(4):
        width = TB * (k + 1)
        first = TB * (k * (k + 1) // 2)
        a_ref[TB * k:TB * (k + 1), 0:width] = pk_ref[:, first:first + width]
    a_ref[PW:end, :] = raw_ref[...]
    for n in range(PW // NB):
        lo, hi = NB * n, NB * (n + 1)
        invert_factor(a_ref[lo:hi, lo:hi], x_ref)
        a_ref[hi:end, lo:hi] = lax.dot_general(
            a_ref[hi:end, lo:hi], x_ref[...], NT, precision=HIGHEST, preferred_element_type=F32)
        for j in range(n + 1, PW // NB):
            jl, jh = NB * j, NB * (j + 1)
            a_ref[jl:end, jl:jh] -= lax.dot_general(
                a_ref[jl:end, lo:hi], a_ref[jl:jh, lo:hi], NT,
                precision=HIGHEST, preferred_element_type=F32)
    solved = a_ref[PW:end, :]
    pf_ref[...] = solved
    pb_ref[...] = solved.astype(BF16)


def factor(packed, raw):
    return pl.pallas_call(
        factor_kernel,
        out_shape=(
            jax.ShapeDtypeStruct((NB, PW), F32), jax.ShapeDtypeStruct((NB, PW), BF16)),
        scratch_shapes=[pltpu.VMEM((PW + NB, PW), F32), pltpu.VMEM((NB, NB), F32)],
        compiler_params=pltpu.CompilerParams(vmem_limit_bytes=48 * MIB),
        name="factor_corner",
    )(packed.reshape(TB, 2560), raw.reshape(NB, PW))


def exchange_kernel(pf_ref, pb_ref, pc_ref, pr_ref, pan_ref, loc, wsend, wrecv, ssem, rsem,
                    zsend, zrecv, csend, crecv, fsend, frecv):
    p, q, x, y, z, c = place()
    here, partner = (p, q), dev(x, y, z, 1 - c)
    twin = (8 * (p // 8) + q, lax.rem(p, 8))
    alone = lax.rem(p, 8) == q
    bar = pltpu.get_barrier_semaphore()
    for d in plane_peers() + [(p, lax.rem(q + i, 8)) for i in range(1, 8)]:
        pl.semaphore_signal(bar, inc=1, device_id=d, device_id_type=MESH)

    @pl.when(alone)
    def _():
        pl.semaphore_wait(bar, 11)

    @pl.when(jnp.logical_not(alone))
    def _():
        pl.semaphore_signal(bar, inc=1, device_id=twin, device_id_type=MESH)
        pl.semaphore_wait(bar, 12)
        remote(pb_ref, pc_ref.at[twin[0]], wsend, wrecv, twin).start()

    mine = pltpu.make_async_copy(pb_ref, pc_ref.at[p], loc.at[0])

    @pl.when(alone)
    def _():
        mine.start()

    keep = pltpu.make_async_copy(pb_ref, pr_ref.at[q], loc.at[1])
    keep.start()

    def over(i):
        return remote(pb_ref, pr_ref.at[q], zsend.at[i - 1], zrecv.at[i - 1],
                      dev(x, y, rem4(z + i), c))

    def across(i):
        src = pb_ref if i == 0 else pr_ref.at[2 * rem4(z - i) + c]
        return remote(src, pr_ref.at[2 * rem4(z - i) + c], csend.at[i], crecv.at[i], partner)

    def block(m):
        return remote(pf_ref.at[:, :, pl.ds(m * TB, TB)], pan_ref.at[q],
                      fsend.at[m], frecv.at[q], (p, m))

    def block_here(m):
        return pltpu.make_async_copy(
            pf_ref.at[:, :, pl.ds(m * TB, TB)], pan_ref.at[q], loc.at[2])

    for i in (1, 3, 2):
        over(i).start()
    across(0).start()
    for m in range(4):
        @pl.when(q != m)
        def _():
            block(m).start()

        @pl.when(q == m)
        def _():
            block_here(m).start()

    plane = Plane(lambda j: pc_ref.at[p, j], lambda s: pc_ref.at[s // 4, lax.rem(s, 4)], ssem, rsem)

    @pl.when(alone)
    def _():
        mine.wait()

    @pl.when(jnp.logical_not(alone))
    def _():
        remote(pb_ref, pc_ref.at[p], wsend, wrecv, twin).wait_recv()

    for n in range(len(COMBOS)):
        plane.event(*COMBOS[n])
        if n in (2, 4, 6):
            i = {2: 1, 4: 3, 6: 2}[n]
            t = pr_ref.at[2 * rem4(z - i) + c]
            remote(t, t, zsend.at[0], zrecv.at[i - 1], here).wait_recv()
            across(i).start()
    plane.drain()
    keep.wait()
    for i in (1, 2, 3):
        over(i).wait_send()
    for i in range(4):
        across(i).wait_send()
        t = pr_ref.at[2 * rem4(z - i) + 1 - c]
        remote(t, t, csend.at[0], crecv.at[i], here).wait_recv()
    for m in range(4):
        @pl.when(q != m)
        def _():
            block(m).wait_send()

        @pl.when(q == m)
        def _():
            block_here(m).wait()
            for i in range(1, 8):
                t = pan_ref.at[lax.rem(q + i, 8)]
                remote(t, t, fsend.at[0], frecv.at[lax.rem(q + i, 8)], here).wait_recv()

    @pl.when(jnp.logical_not(alone))
    def _():
        remote(pb_ref, pc_ref.at[p], wsend, wrecv, twin).wait_send()


def exchange(pf, pb):
    hbm = pl.BlockSpec(memory_space=pl.ANY)
    return pl.pallas_call(
        exchange_kernel,
        out_shape=(
            jax.ShapeDtypeStruct((16, 4, 32, PW), BF16),
            jax.ShapeDtypeStruct((8, 4, 32, PW), BF16),
            jax.ShapeDtypeStruct((8, 16, 8, TB), F32),
        ),
        in_specs=[hbm, hbm],
        out_specs=(hbm, hbm, hbm),
        scratch_shapes=[
            DMA((3,)), DMA(()), DMA(()), DMA((60,)), DMA((64,)), DMA((3,)), DMA((3,)),
            DMA((4,)), DMA((4,)), DMA((4,)), DMA((8,)),
        ],
        compiler_params=pltpu.CompilerParams(collective_id=2, has_side_effects=True),
        name="exchange_panel",
    )(pf.reshape(16, 8, PW), pb.reshape(4, 32, PW))


STRIP = 128


def update_kernel(s_ref, pr_ref, pc_ref, pan_ref, out_ref):
    p, q = lax.axis_index("scen"), lax.axis_index("col")
    a = pl.program_id(0) // (TB // STRIP)
    low = jnp.logical_or(a > 0, p >= 4)
    panel = q < 4
    for b in range(8):
        cols = slice(b * TB, (b + 1) * TB)
        first = (b % 2) * 1024 + (b // 2) * TB

        def lowered():
            out_ref[:, cols] = s_ref[:, cols] - lax.dot_general(
                pr_ref[...], pc_ref[first:first + TB, :], NT, preferred_element_type=F32)

        def kept():
            out_ref[:, cols] = s_ref[:, cols]

        def solved():
            out_ref[:, cols] = pan_ref[...]

        if b == 0:
            pl.when(panel)(solved)
            pl.when(jnp.logical_and(jnp.logical_not(panel), low))(lowered)
            pl.when(jnp.logical_and(jnp.logical_not(panel), jnp.logical_not(low)))(kept)
        else:
            pl.when(low)(lowered)
            pl.when(jnp.logical_not(low))(kept)


def update(schur, rows, cols, panel):
    strip = pl.BlockSpec((STRIP, 2048), lambda i: (i, 0))
    return pl.pallas_call(
        update_kernel,
        out_shape=jax.ShapeDtypeStruct((1024, 2048), F32),
        grid=(1024 // STRIP,),
        in_specs=[
            strip,
            pl.BlockSpec((STRIP, PW), lambda i: (i, 0)),
            pl.BlockSpec((2048, PW), lambda i: (0, 0)),
            pl.BlockSpec((STRIP, TB), lambda i: (i, 0)),
        ],
        out_specs=strip,
        compiler_params=pltpu.CompilerParams(vmem_limit_bytes=48 * MIB),
        name="update",
    )(schur, rows.reshape(1024, PW), cols.reshape(2048, PW), panel.reshape(1024, TB))


def per_device(border, touched, barrier):
    gathered, rows = gather_borders(border)
    schur = assemble(touched, gathered, rows, barrier)
    packed, raw = spread(schur)
    solved, rounded = factor(packed, raw)
    panel_cols, panel_rows, panel = exchange(solved, rounded)
    return update(schur, panel_rows, panel_cols, panel)


def solution(mesh):
    in_specs = (P("scen", None, "col"), P(), P())
    out_specs = P("scen", "col")
    return jax.shard_map(
        per_device, mesh=mesh, in_specs=in_specs, out_specs=out_specs, check_vma=False
    )
```

```python
import jax
import jax.numpy as jnp
from jax import lax
from jax.experimental import pallas as pl
from jax.experimental.pallas import tpu as pltpu
from jax.sharding import PartitionSpec as P

N = 16384
TB = 256
KT = 8
PW = 1024
SCEN = 64
NB = 128
F32 = jnp.float32
BF16 = jnp.bfloat16
HIGHEST = lax.Precision.HIGHEST
MESH = pl.DeviceIdType.MESH
DMA = pltpu.SemaphoreType.DMA
NT = (((1,), (1,)), ((), ()))
TN = (((0,), (0,)), ((), ()))
MIB = 1024 * 1024

COMBOS = [
    (0, 0), (1, 0), (3, 0), (0, 1), (0, 3), (2, 0), (0, 2), (1, 1),
    (1, 3), (3, 1), (3, 3), (2, 1), (2, 3), (1, 2), (3, 2), (2, 2),
]


def plane_slots():
    slots = {}
    for e1, e2 in COMBOS:
        if e2 == 0:
            kinds = {0: (0, 1, 2, 3), 1: (0, 2, 3)}.get(e1, (2, 3))
        else:
            kinds = (2,) if e2 == 1 else ()
        for kind in kinds:
            slots[(e1, e2, kind)] = len(slots)
    return slots


SLOTS = plane_slots()


def rem4(v):
    return lax.rem(v + 8, 4)


def place():
    p = lax.axis_index("scen")
    q = lax.axis_index("col")
    return p, q, p // 4, lax.rem(p, 4), q // 2, lax.rem(q, 2)


def dev(x, y, z, c):
    return (x * 4 + y, z * 2 + c)


def remote(src, dst, send, recv, device):
    return pltpu.make_async_remote_copy(
        src_ref=src, dst_ref=dst, send_sem=send, recv_sem=recv,
        device_id=device, device_id_type=MESH,
    )


def greet(devices):
    bar = pltpu.get_barrier_semaphore()
    for d in devices:
        pl.semaphore_signal(bar, inc=1, device_id=d, device_id_type=MESH)
    pl.semaphore_wait(bar, len(devices))


def lane(v):
    return pl.multiple_of(v, 128)


class Plane:
    def __init__(self, own, tiles, send_sem, recv_sem):
        self.own, self.tiles = own, tiles
        self.send_sem, self.recv_sem = send_sem, recv_sem
        self.p, self.q, self.x, self.y, self.z, self.c = place()

    def geom(self, j):
        return 1 - j, j, 1 - 2 * j

    def tile(self, e1, e2, j):
        sx, sy, _ = self.geom(j)
        ox = rem4(self.x - e1 * sx + e2 * sy)
        oy = rem4(self.y - e1 * sy + e2 * sx)
        return 2 * (ox * 4 + oy) + j

    def event(self, e1, e2, extra=None):
        def body(j, _):
            sx, sy, d = self.geom(j)
            s = self.tile(e1, e2, j)
            dst = self.tiles(s)
            if (e1, e2) == (0, 0):
                src = self.own(j)
            else:
                src = dst
                remote(
                    src, src, self.send_sem.at[0],
                    self.recv_sem.at[(e1 * 4 + e2) * 2 + j], (self.p, self.q),
                ).wait_recv()

            def send(kind, first, sign, r1, r2):
                dx = sx * sign if first else -sy * sign
                dy = sy * sign if first else -sx * sign
                remote(
                    src, dst, self.send_sem.at[SLOTS[(e1, e2, kind)] * 2 + j],
                    self.recv_sem.at[(r1 * 4 + r2) * 2 + j],
                    dev(rem4(self.x + dx), rem4(self.y + dy), self.z, self.c),
                ).start()

            if e2 == 0:
                if e1 == 0:
                    send(0, True, 1, 1, 0)
                    send(1, True, -1, 3, 0)
                if e1 == 1:
                    send(0, True, 1, 2, 0)
                send(2, False, 1, e1, 1)
                send(3, False, -1, e1, 3)
            elif e2 == 1:
                send(2, False, 1, e1, 2)
            if extra is not None:
                extra(src, s, (e1 * 4 + e2) * 2 + j, d)
            return 0

        lax.fori_loop(0, 2, body, 0)

    def drain(self):
        t = self.tiles(0)

        def body(i, _):
            remote(t, t, self.send_sem.at[i], self.recv_sem.at[0], (self.p, self.q)).wait_send()
            return 0

        lax.fori_loop(0, 2 * len(SLOTS), body, 0)


def plane_peers():
    p, q, x, y, z, c = place()
    return [
        dev(rem4(x + 1), y, z, c), dev(rem4(x - 1), y, z, c),
        dev(x, rem4(y + 1), z, c), dev(x, rem4(y - 1), z, c),
    ]


def relay_steps(plane, h_ref, zsem, psem, hsem):
    p, q, x, y, z, c = place()
    k = lax.rem(p, 8)
    zs, cs = k // 2, lax.rem(k, 2)
    here, partner = (p, q), dev(x, y, z, 1 - c)
    chain = c == cs
    source = jnp.logical_and(chain, z == zs)

    def feed(src, s, h, d):
        @pl.when(source)
        def _():
            remote(src, h_ref.at[s], zsem.at[h], hsem.at[h], dev(x, y, rem4(z + d), c)).start()
            remote(src, h_ref.at[s], psem.at[h], hsem.at[h], partner).start()

    def relay(e1, e2, r):
        def body(j, _):
            d = 1 - 2 * j
            h = (e1 * 4 + e2) * 2 + j

            @pl.when(jnp.logical_and(chain, rem4((z - zs) * d) == r))
            def _():
                t = h_ref.at[plane.tile(e1, e2, j)]
                remote(t, t, zsem.at[0], hsem.at[h], here).wait_recv()
                if r < 3:
                    remote(t, t, zsem.at[h], hsem.at[h], dev(x, y, rem4(z + d), c)).start()
                remote(t, t, psem.at[h], hsem.at[h], partner).start()

            return 0

        lax.fori_loop(0, 2, body, 0)

    def step(n):
        if n < len(COMBOS):
            plane.event(*COMBOS[n], extra=feed)
        for r in (1, 2, 3):
            if 0 <= n - r < len(COMBOS):
                relay(*COMBOS[n - r], r)

    def drain():
        t = h_ref.at[0]

        def last(i, _):
            d = 1 - 2 * lax.rem(i, 2)

            @pl.when(jnp.logical_and(chain, rem4((z - zs) * d) < 3))
            def _():
                remote(t, t, zsem.at[i], hsem.at[0], here).wait_send()

            @pl.when(chain)
            def _():
                remote(t, t, psem.at[i], hsem.at[0], here).wait_send()

            @pl.when(jnp.logical_not(chain))
            def _():
                remote(t, t, zsem.at[0], hsem.at[i], here).wait_recv()

            return 0

        lax.fori_loop(0, SCEN // 2, last, 0)

    return [lambda n=n: step(n) for n in range(len(COMBOS) + 3)], drain


PARTS = {
    (0, 0): [(0, 2)], (1, 0): [(0, 3), (1, 3)], (1, 1): [(1, 2)],
    (2, 0): [(0, 0), (2, 0)], (2, 1): [(0, 1), (3, 0)], (2, 2): [(2, 2)],
    (3, 0): [(1, 0), (2, 1)], (3, 1): [(1, 1), (3, 1)], (3, 2): [(2, 3), (3, 3)],
    (3, 3): [(3, 2)],
}


PACE = (1, 1, 1, 1, 1, 1, 1, 1)


def front_kernel(b_ref, bm_ref, bar_ref, g_ref, h_ref, w_ref,
                 xb, xc, part, rbuf, fin, zb, pk, v_ref,
                 loc, s1, r1, s2, r2, s3, r3, s4, r4, s5, r5,
                 ssem, rsem, zsem, psem, hsem):
    p, q, x, y, z, c = place()
    here, partner = (p, q), dev(x, y, z, 1 - c)
    greet([(lax.rem(p + i, 16), q) for i in range(1, 16)]
          + [(p, lax.rem(q + i, 8)) for i in range(1, 8)])
    own = pltpu.make_async_copy(b_ref, g_ref.at[pl.ds(2 * p, 2)], loc)
    own.start()
    plane = Plane(lambda j: b_ref.at[j], lambda s: g_ref.at[s], ssem, rsem)
    steps, drain = relay_steps(plane, h_ref, zsem, psem, hsem)

    def go(spot):
        for _ in range(min(len(steps), PACE[spot])):
            steps.pop(0)()

    go(0)
    holds = q < 4
    facing = dev(x, y, lax.rem(z + 1, 2), c)

    def to_partner():
        return remote(bm_ref, xb, s1.at[0], r1.at[0], partner)

    def to_facing():
        return remote(bm_ref.at[pl.ds(2 * lax.rem(z, 2), 2)], xc, s1.at[1], r1.at[1], facing)

    def slab(v):
        return v.reshape(v.shape[0] * TB, TB)

    def product(left, right):
        return lax.dot_general(slab(left), slab(right), TN, preferred_element_type=F32)

    def put(t, tile):
        part[:, t] = tile.reshape(16, 16, TB)

    def slices(i):
        g = lax.rem(p + i, 16)
        return remote(part.at[g], rbuf.at[p], s2.at[i - 1], r2.at[i - 1], (g, q))

    def halves(i):
        to = lax.rem(q + i, 8)
        return remote(fin.at[lax.rem(to, 2)], zb.at[q], s3.at[i - 1], r3.at[q], (p, to))

    @pl.when(holds)
    def _():
        to_facing().start()
        to_partner().start()
        put(2, product(bm_ref[...], bm_ref[...]))
        to_partner().wait_recv()

        def both(first, second):
            sl = pl.ds(2 * c, 2)
            put(3, product(second[sl], first[sl]))
            to_facing().wait_recv()

            @pl.when(z == 0)
            def _():
                put(0, product(xc[...], first[2:4]))
                put(1, product(xc[...], second[2:4]))

            @pl.when(z == 1)
            def _():
                put(0, product(first[0:2], xc[...]))
                put(1, product(second[0:2], xc[...]))

        @pl.when(c == 0)
        def _():
            both(bm_ref, xb)

        @pl.when(c == 1)
        def _():
            both(xb, bm_ref)

        for i in range(1, 16):
            slices(i).start()
        rbuf[p] = part[p]

    go(1)

    @pl.when(holds)
    def _():
        for i in range(1, 16):
            t = rbuf.at[lax.rem(p + 16 - i, 16)]
            remote(t, t, s2.at[i - 1], r2.at[i - 1], here).wait_recv()
        total = rbuf[0]
        for i in range(1, 16):
            total = total + rbuf[i]
        fin[0] = total[:, 0:8]
        fin[1] = total[:, 8:16]
        for i in range(1, 8):
            halves(i).start()
        zb[lax.rem(q, 4)] = fin[c]

    go(2)
    for m in range(4):
        @pl.when(q != m)
        def _():
            remote(zb.at[m], zb.at[m], s3.at[0], r3.at[m], here).wait_recv()

    at = (lax.broadcasted_iota(jnp.int32, (8, TB), 1)
          == p * 16 + c * 8 + lax.broadcasted_iota(jnp.int32, (8, TB), 0))
    for (k, m), parts in PARTS.items():
        v = zb[parts[0][0], parts[0][1]]
        for owner, t in parts[1:]:
            v = v + zb[owner, t]
        if k == m:
            v = v + jnp.where(at, bar_ref[k:k + 1, :], 0.0)
        first = (k * (k + 1) // 2 + m) * TB
        pk[p, c, :, first:first + TB] = v

    def shard(i):
        return remote(pk.at[p, c], pk.at[p, c], s4.at[i - 1], r4.at[i - 1],
                      (lax.rem(p + i, 16), q))

    def pass_on(i):
        t = pk.at[lax.rem(p + 16 - i, 16), c]
        return remote(t, t, s5.at[i], r5.at[i], partner)

    for i in range(1, 16):
        shard(i).start()
    pass_on(0).start()
    go(3)
    for i in range(1, 16):
        t = pk.at[lax.rem(p + 16 - i, 16), c]
        remote(t, t, s4.at[i - 1], r4.at[i - 1], here).wait_recv()
        pass_on(i).start()
        if i % 5 == 0:
            go(3 + i // 5)
    for i in range(16):
        t = pk.at[lax.rem(p + 16 - i, 16), 1 - c]
        remote(t, t, s5.at[i], r5.at[i], here).wait_recv()

    for k in range(4):
        width = TB * (k + 1)
        first = TB * (k * (k + 1) // 2)
        w_ref[TB * k:TB * (k + 1), 0:width] = pk[:, :, :, first:first + width].reshape(TB, width)
    blocks = PW // NB

    for n in range(blocks):
        lo, hi = NB * n, NB * (n + 1)
        turned = invert_factor(w_ref[lo:hi, lo:hi]).T
        go(7)
        v = jnp.dot(left_parts(w_ref[:, lo:hi]), right_parts(turned, 0),
                    preferred_element_type=F32)
        w_ref[:, lo:hi] = v
        w_ref[lo:hi, lo:hi] = turned
        if hi < PW:
            v_ref[...] = left_parts(w_ref[:, lo:hi])
            below = right_parts(w_ref[hi:PW, lo:hi], 1)
            w_ref[lo:hi, hi:PW] = jnp.zeros((NB, PW - hi), F32)
            for jl in range(hi, PW, TB):
                jh = min(jl + TB, PW)
                w_ref[:, jl:jh] -= lax.dot_general(
                    v_ref[...], below[jl - hi:jh - hi], NT, preferred_element_type=F32)
        go(7)
    while steps:
        steps.pop(0)()

    own.wait()
    plane.drain()
    drain()

    @pl.when(holds)
    def _():
        to_partner().wait_send()
        to_facing().wait_send()
        for i in range(1, 16):
            slices(i).wait_send()
        for i in range(1, 8):
            halves(i).wait_send()

    for i in range(1, 16):
        shard(i).wait_send()
    for i in range(16):
        pass_on(i).wait_send()


def front(border, masked, barrier):
    tiles = jax.ShapeDtypeStruct((SCEN // 2, 2, TB, TB), BF16)
    hbm = pl.BlockSpec(memory_space=pl.ANY)
    vmem = pl.BlockSpec(memory_space=pltpu.VMEM)
    return pl.pallas_call(
        front_kernel,
        out_shape=(tiles, tiles, jax.ShapeDtypeStruct((PW, PW), F32)),
        in_specs=[hbm, vmem, vmem],
        out_specs=(hbm, hbm, vmem),
        scratch_shapes=[
            pltpu.VMEM((4, TB, TB), BF16), pltpu.VMEM((2, TB, TB), BF16),
            pltpu.VMEM((16, 4, 16, TB), F32), pltpu.VMEM((16, 4, 16, TB), F32),
            pltpu.VMEM((2, 4, 8, TB), F32), pltpu.VMEM((4, 4, 8, TB), F32),
            pltpu.VMEM((16, 2, 8, 2560), F32), pltpu.VMEM((PW, 6 * NB), BF16),
            DMA(()), DMA((2,)), DMA((2,)), DMA((15,)), DMA((15,)), DMA((7,)), DMA((4,)),
            DMA((15,)), DMA((15,)), DMA((16,)), DMA((16,)),
            DMA((30,)), DMA((32,)), DMA((32,)), DMA((32,)), DMA((32,)),
        ],
        compiler_params=pltpu.CompilerParams(
            collective_id=0, has_side_effects=True, vmem_limit_bytes=48 * MIB),
        name="front",
    )(border.reshape(2, 2, TB, TB), masked, barrier)


PER_STEP = 4


def schur_kernel(touched_ref, g_ref, h_ref, bar_ref, out_ref):
    p, q = lax.axis_index("scen"), lax.axis_index("col")
    k = lax.rem(p, 8)
    step = pl.program_id(0)
    diagonal = k == q

    @pl.when(step == 0)
    def _():
        out_ref[...] = jnp.zeros_like(out_ref)

        @pl.when(diagonal)
        def _():
            eye = lax.broadcasted_iota(jnp.int32, (TB, TB), 0) == lax.broadcasted_iota(
                jnp.int32, (TB, TB), 1
            )
            for a in range(4):
                col = lane((2 * a + p // 8) * TB)
                row = bar_ref[pl.ds(a * 16 + p, 1), :]
                out_ref[a * TB:(a + 1) * TB, pl.ds(col, TB)] = jnp.where(eye, row, 0.0)

    for i in range(PER_STEP):
        s = step * PER_STEP + i
        big_row = touched_ref[s * KT + k]

        @pl.when(lax.rem(big_row, 16) == p)
        def _():
            row = pl.multiple_of((big_row // 16) * TB, TB)
            col = lane((touched_ref[s * KT + q] // 8) * TB)
            left = jnp.where(diagonal, g_ref[i], h_ref[i])
            out_ref[pl.ds(row, TB), pl.ds(col, TB)] += lax.dot_general(
                left, g_ref[i], TN, preferred_element_type=F32
            )


def assemble(touched, gathered, rows, barrier):
    block = pl.BlockSpec((PER_STEP, TB, TB), lambda i, t: (i, 0, 0))
    return pl.pallas_call(
        schur_kernel,
        out_shape=jax.ShapeDtypeStruct((1024, 2048), F32),
        grid_spec=pltpu.PrefetchScalarGridSpec(
            num_scalar_prefetch=1,
            grid=(SCEN // PER_STEP,),
            in_specs=[block, block, pl.BlockSpec((N // TB, TB), lambda i, t: (0, 0))],
            out_specs=pl.BlockSpec((1024, 2048), lambda i, t: (0, 0)),
        ),
        compiler_params=pltpu.CompilerParams(vmem_limit_bytes=48 * MIB),
        name="assemble",
    )(touched.reshape(-1), gathered.reshape(SCEN, TB, TB), rows.reshape(SCEN, TB, TB),
      barrier.reshape(N // TB, TB))


def pivot_pair(a, b, d):
    q0 = lax.rsqrt(a)
    q1 = lax.rsqrt(a * (a * d - b * b))
    inv = q1 * q1 * a
    return q0, q1, d * inv, b * inv, a * inv


def pivot_four(w):
    (w00,), (w10, w11), (w20, w21, w22), (w30, w31, w32, w33) = w
    q0, q1, ci, bi, ai = pivot_pair(w00, w10, w11)
    e02, e12 = ci * w20 - bi * w21, ai * w21 - bi * w20
    e03, e13 = ci * w30 - bi * w31, ai * w31 - bi * w30
    v22 = w22 - w20 * e02 - w21 * e12
    v32 = w32 - w30 * e02 - w31 * e12
    v33 = w33 - w30 * e03 - w31 * e13
    q2, q3, cj, bj, aj = pivot_pair(v22, v32, v33)

    def solve(r0, r1, r2, r3):
        z0, z1 = ci * r0 - bi * r1, ai * r1 - bi * r0
        s2, s3 = r2 - w20 * z0 - w21 * z1, r3 - w30 * z0 - w31 * z1
        z2, z3 = cj * s2 - bj * s3, aj * s3 - bj * s2
        return z0 - e02 * z2 - e03 * z3, z1 - e12 * z2 - e13 * z3, z2, z3, s2, s3

    def half(r0, r1, s2, s3):
        return [r0 * q0, (w00 * r1 - w10 * r0) * q1, s2 * q2, (v22 * s3 - v32 * s2) * q3]

    return solve, half


def splat(row, at):
    return jnp.broadcast_to(row[:, at:at + 1], (1, NB))


HB = NB // 2


def small_inverse(a):
    eye = (
        lax.broadcasted_iota(jnp.int32, (HB, HB), 0)
        == lax.broadcasted_iota(jnp.int32, (HB, HB), 1)
    ).astype(F32)
    t = jnp.concatenate([a, eye], axis=1)
    top, rows, w = 0, [], None
    for o in range(0, HB, 4):
        if 8 * (o // 8) > top:
            t, top = t[8 * (o // 8) - top:], 8 * (o // 8)
        k, height = o - top, t.shape[0]
        c = [jnp.broadcast_to(t[:, o + i:o + i + 1], (height, NB)) for i in range(4)]
        r = [t[k + i:k + i + 1, :] for i in range(4)]
        if w is None:
            w = [[c[v][k + u:k + u + 1, :] for v in range(u + 1)] for u in range(4)]
        solve, half = pivot_four(w)
        last = o + 4 == HB
        if not last:
            after = [t[k + 4 + i:k + 5 + i, :] for i in range(4)]
            g = [[splat(r[i], o + 4 + u) for u in range(4)] for i in range(4)]
            z = [solve(*[g[i][v] for i in range(4)]) for v in range(4)]
            w = [[splat(after[u], o + 4 + v)
                  - (g[0][u] * z[v][0] + g[1][u] * z[v][1])
                  - (g[2][u] * z[v][2] + g[3][u] * z[v][3]) for v in range(u + 1)]
                 for u in range(4)]
        z0, z1, z2, z3, s2, s3 = solve(*r)
        rows += half(r[0], r[1], s2, s3)
        if not last:
            t = t - (c[0] * z0 + c[1] * z1) - (c[2] * z2 + c[3] * z3)
    return jnp.concatenate(rows, 0)[:, HB:NB]


def wide(a, b, dims=(((1,), (0,)), ((), ()))):
    return lax.dot_general(a, b, dims, precision=HIGHEST, preferred_element_type=F32)


def thirds(v):
    a = v.astype(BF16)
    rest = v - a.astype(F32)
    b = rest.astype(BF16)
    return a, b, (rest - b.astype(F32)).astype(BF16)


def left_parts(v):
    a, b, c = thirds(v)
    return jnp.concatenate([a, a, b, b, a, c], axis=1)


def right_parts(v, axis):
    a, b, c = thirds(v)
    return jnp.concatenate([a, b, a, b, c, a], axis=axis)


def invert_factor(a):
    x1 = small_inverse(a[:HB, :HB])
    l = wide(a[HB:, :HB], x1, NT)
    x2 = small_inverse(a[HB:, HB:] - wide(l, l, NT))
    x21 = -wide(wide(x2, l), x1)
    return jnp.concatenate([
        jnp.concatenate([x1, jnp.zeros((HB, HB), F32)], 1),
        jnp.concatenate([x21, x2], 1)], 0)


def panel_kernel(s_ref, w_hbm, pc_ref, pr_ref, pan_ref, w_ref, raw_ref, pf_ref, pb_ref,
                 loc, asend, arecv, wsend, wrecv, ssem, rsem,
                 zsend, zrecv, csend, crecv, fsend, frecv):
    p, q, x, y, z, c = place()
    here, partner = (p, q), dev(x, y, z, 1 - c)
    twin = (8 * (p // 8) + q, lax.rem(p, 8))
    alone = lax.rem(p, 8) == q
    bar = pltpu.get_barrier_semaphore()
    for d in plane_peers() + [(p, lax.rem(q + i, 8)) for i in range(1, 8)]:
        pl.semaphore_signal(bar, inc=1, device_id=d, device_id_type=MESH)

    @pl.when(alone)
    def _():
        pl.semaphore_wait(bar, 11)

    @pl.when(jnp.logical_not(alone))
    def _():
        pl.semaphore_signal(bar, inc=1, device_id=twin, device_id_type=MESH)
        pl.semaphore_wait(bar, 12)

    holds = q < 4
    mine = lane(lax.rem(q, 4) * TB)

    def rows_to(i):
        to = lax.rem(q + i, 8)
        return remote(s_ref.at[pl.ds(16 * to, 16), :, pl.ds(0, TB)],
                      raw_ref.at[:, :, pl.ds(mine, TB)],
                      asend.at[i - 1], arecv.at[lax.rem(q, 4)], (p, to))

    own_rows = pltpu.make_async_copy(
        s_ref.at[pl.ds(16 * q, 16), :, pl.ds(0, TB)], raw_ref.at[:, :, pl.ds(mine, TB)], loc.at[0])
    inverse = pltpu.make_async_copy(w_hbm, w_ref, loc.at[1])

    @pl.when(holds)
    def _():
        for i in (2, 3, 4, 5, 6, 1, 7):
            rows_to(i).start()
        own_rows.start()

    inverse.start()
    for m in range(4):
        @pl.when(q == m)
        def _():
            own_rows.wait()

        @pl.when(q != m)
        def _():
            t = raw_ref.at[:, :, pl.ds(m * TB, TB)]
            remote(t, t, asend.at[0], arecv.at[m], here).wait_recv()

    inverse.wait()
    for n in range(PW // NB):
        lo, hi = NB * n, NB * (n + 1)
        v = jnp.dot(raw_ref[:, :, 0:hi].reshape(NB, hi), w_ref[0:hi, lo:hi],
                    precision=HIGHEST, preferred_element_type=F32)
        pf_ref[:, :, lo:hi] = v.reshape(16, 8, NB)
        pb_ref[:, :, lo:hi] = v.astype(BF16).reshape(2, 64, NB)

    def to_twin():
        return remote(pb_ref, pc_ref.at[twin[0]], wsend, wrecv, twin)

    keep_cols = pltpu.make_async_copy(pb_ref, pc_ref.at[p], loc.at[2])
    keep_rows = pltpu.make_async_copy(pb_ref, pr_ref.at[q], loc.at[3])

    @pl.when(alone)
    def _():
        keep_cols.start()

    @pl.when(jnp.logical_not(alone))
    def _():
        to_twin().start()

    keep_rows.start()

    def over(i):
        return remote(pb_ref, pr_ref.at[q], zsend.at[i - 1], zrecv.at[i - 1],
                      dev(x, y, rem4(z + i), c))

    def across(i):
        src = pb_ref if i == 0 else pr_ref.at[2 * rem4(z - i) + c]
        return remote(src, pr_ref.at[2 * rem4(z - i) + c], csend.at[i], crecv.at[i], partner)

    def block(m):
        return remote(pf_ref.at[:, :, pl.ds(m * TB, TB)], pan_ref.at[q],
                      fsend.at[m], frecv.at[q], (p, m))

    def block_here(m):
        return pltpu.make_async_copy(
            pf_ref.at[:, :, pl.ds(m * TB, TB)], pan_ref.at[q], loc.at[4])

    plane = Plane(lambda j: pc_ref.at[p, j], lambda s: pc_ref.at[s // 2, lax.rem(s, 2)], ssem, rsem)

    @pl.when(alone)
    def _():
        keep_cols.wait()

    @pl.when(jnp.logical_not(alone))
    def _():
        remote(pb_ref, pc_ref.at[p], wsend, wrecv, twin).wait_recv()

    for n in range(len(COMBOS)):
        plane.event(*COMBOS[n])
        if n == 0:
            for i in (1, 3, 2):
                over(i).start()
            across(0).start()
            for m in range(4):
                @pl.when(q != m)
                def _():
                    block(m).start()

                @pl.when(q == m)
                def _():
                    block_here(m).start()
        if n in (4, 6, 8):
            i = {4: 1, 6: 3, 8: 2}[n]
            t = pr_ref.at[2 * rem4(z - i) + c]
            remote(t, t, zsend.at[0], zrecv.at[i - 1], here).wait_recv()
            across(i).start()
    plane.drain()
    keep_rows.wait()
    for i in (1, 2, 3):
        over(i).wait_send()
    for i in range(4):
        across(i).wait_send()
        t = pr_ref.at[2 * rem4(z - i) + 1 - c]
        remote(t, t, csend.at[0], crecv.at[i], here).wait_recv()
    for m in range(4):
        @pl.when(q != m)
        def _():
            block(m).wait_send()

        @pl.when(q == m)
        def _():
            block_here(m).wait()
            for i in range(1, 8):
                t = pan_ref.at[lax.rem(q + i, 8)]
                remote(t, t, fsend.at[0], frecv.at[lax.rem(q + i, 8)], here).wait_recv()

    @pl.when(jnp.logical_not(alone))
    def _():
        to_twin().wait_send()

    @pl.when(holds)
    def _():
        for i in range(1, 8):
            rows_to(i).wait_send()


def solve_panel(schur, inverse):
    hbm = pl.BlockSpec(memory_space=pl.ANY)
    return pl.pallas_call(
        panel_kernel,
        out_shape=(
            jax.ShapeDtypeStruct((16, 2, 64, PW), BF16),
            jax.ShapeDtypeStruct((8, 2, 64, PW), BF16),
            jax.ShapeDtypeStruct((8, 16, 8, TB), F32),
        ),
        in_specs=[hbm, hbm],
        out_specs=(hbm, hbm, hbm),
        scratch_shapes=[
            pltpu.VMEM((PW, PW), F32), pltpu.VMEM((16, 8, PW), F32),
            pltpu.VMEM((16, 8, PW), F32), pltpu.VMEM((2, 64, PW), BF16),
            DMA((5,)), DMA((7,)), DMA((4,)), DMA(()), DMA(()), DMA((30,)), DMA((32,)),
            DMA((3,)), DMA((3,)), DMA((4,)), DMA((4,)), DMA((4,)), DMA((8,)),
        ],
        compiler_params=pltpu.CompilerParams(
            collective_id=1, has_side_effects=True, vmem_limit_bytes=32 * MIB),
        name="solve_panel",
    )(schur.reshape(128, 8, 2048), inverse)


STRIP = 128


def update_kernel(s_ref, pr_ref, pc_ref, pan_ref, out_ref):
    p, q = lax.axis_index("scen"), lax.axis_index("col")
    a = pl.program_id(0) // (TB // STRIP)
    low = jnp.logical_or(a > 0, p >= 4)
    panel = q < 4
    for b in range(8):
        cols = slice(b * TB, (b + 1) * TB)
        first = (b % 2) * 1024 + (b // 2) * TB

        def lowered():
            out_ref[:, cols] = s_ref[:, cols] - lax.dot_general(
                pr_ref[...], pc_ref[first:first + TB, :], NT, preferred_element_type=F32)

        def kept():
            out_ref[:, cols] = s_ref[:, cols]

        def solved():
            out_ref[:, cols] = pan_ref[...]

        if b == 0:
            pl.when(panel)(solved)
            pl.when(jnp.logical_and(jnp.logical_not(panel), low))(lowered)
            pl.when(jnp.logical_and(jnp.logical_not(panel), jnp.logical_not(low)))(kept)
        else:
            pl.when(low)(lowered)
            pl.when(jnp.logical_not(low))(kept)


def update(schur, rows, cols, panel):
    strip = pl.BlockSpec((STRIP, 2048), lambda i: (i, 0))
    return pl.pallas_call(
        update_kernel,
        out_shape=jax.ShapeDtypeStruct((1024, 2048), F32),
        grid=(1024 // STRIP,),
        in_specs=[
            strip,
            pl.BlockSpec((STRIP, PW), lambda i: (i, 0)),
            pl.BlockSpec((2048, PW), lambda i: (0, 0)),
            pl.BlockSpec((STRIP, TB), lambda i: (i, 0)),
        ],
        out_specs=strip,
        compiler_params=pltpu.CompilerParams(vmem_limit_bytes=48 * MIB),
        name="update",
    )(schur, rows.reshape(1024, PW), cols.reshape(2048, PW), panel.reshape(1024, TB))


def per_device(border, touched, barrier):
    p, q = lax.axis_index("scen"), lax.axis_index("col")
    mine = lax.dynamic_slice(touched, (4 * p, q), (4, 1))
    masked = jnp.where((mine == q)[:, :, None], border, jnp.zeros_like(border))
    gathered, rows, inverse = front(border, masked, barrier[:PW].reshape(4, TB))
    schur = assemble(touched, gathered, rows, barrier)
    panel_cols, panel_rows, panel = solve_panel(schur, inverse)
    return update(schur, panel_rows, panel_cols, panel)


def solution(mesh):
    in_specs = (P("scen", None, "col"), P(), P())
    out_specs = P("scen", "col")
    return jax.shard_map(
        per_device, mesh=mesh, in_specs=in_specs, out_specs=out_specs, check_vma=False
    )
```

```python
import jax
import jax.numpy as jnp
from jax import lax
from jax.experimental import pallas as pl
from jax.experimental.pallas import tpu as pltpu
from jax.sharding import PartitionSpec as P

N = 16384
TB = 256
KT = 8
PW = 1024
SCEN = 64
NB = 128
F32 = jnp.float32
BF16 = jnp.bfloat16
HIGHEST = lax.Precision.HIGHEST
MESH = pl.DeviceIdType.MESH
DMA = pltpu.SemaphoreType.DMA
NT = (((1,), (1,)), ((), ()))
TN = (((0,), (0,)), ((), ()))
MIB = 1024 * 1024

COMBOS = [
    (0, 0), (1, 0), (3, 0), (0, 1), (0, 3), (2, 0), (0, 2), (1, 1),
    (1, 3), (3, 1), (3, 3), (2, 1), (2, 3), (1, 2), (3, 2), (2, 2),
]


def plane_slots():
    slots = {}
    for e1, e2 in COMBOS:
        if e2 == 0:
            kinds = {0: (0, 1, 2, 3), 1: (0, 2, 3)}.get(e1, (2, 3))
        else:
            kinds = (2,) if e2 == 1 else ()
        for kind in kinds:
            slots[(e1, e2, kind)] = len(slots)
    return slots


SLOTS = plane_slots()


def rem4(v):
    return lax.rem(v + 8, 4)


def place():
    p = lax.axis_index("scen")
    q = lax.axis_index("col")
    return p, q, p // 4, lax.rem(p, 4), q // 2, lax.rem(q, 2)


def dev(x, y, z, c):
    return (x * 4 + y, z * 2 + c)


def remote(src, dst, send, recv, device):
    return pltpu.make_async_remote_copy(
        src_ref=src, dst_ref=dst, send_sem=send, recv_sem=recv,
        device_id=device, device_id_type=MESH,
    )


def greet(devices):
    bar = pltpu.get_barrier_semaphore()
    for d in devices:
        pl.semaphore_signal(bar, inc=1, device_id=d, device_id_type=MESH)
    pl.semaphore_wait(bar, len(devices))


def lane(v):
    return pl.multiple_of(v, 128)


class Plane:
    def __init__(self, count, own, tiles, send_sem, recv_sem):
        self.count = count
        self.own, self.tiles = own, tiles
        self.send_sem, self.recv_sem = send_sem, recv_sem
        self.p, self.q, self.x, self.y, self.z, self.c = place()

    def geom(self, j):
        if self.count == 2:
            return 1 - j, j, 1, -1
        sy = j // 2
        d = 1 - 2 * lax.rem(j, 2)
        return 1 - sy, sy, d, d

    def tile(self, e1, e2, j):
        sx, sy, d1, d2 = self.geom(j)
        ox = rem4(self.x - d1 * e1 * sx - d2 * e2 * sy)
        oy = rem4(self.y - d1 * e1 * sy - d2 * e2 * sx)
        return self.count * (ox * 4 + oy) + j

    def event(self, e1, e2, extra=None):
        def body(j, _):
            sx, sy, d1, d2 = self.geom(j)
            s = self.tile(e1, e2, j)
            dst = self.tiles(s)
            if (e1, e2) == (0, 0):
                src = self.own(j)
            else:
                src = dst
                remote(
                    src, src, self.send_sem.at[0],
                    self.recv_sem.at[(e1 * 4 + e2) * self.count + j], (self.p, self.q),
                ).wait_recv()

            def send(kind, first, sign, r1, r2):
                dx = sx * d1 * sign if first else sy * d2 * sign
                dy = sy * d1 * sign if first else sx * d2 * sign
                remote(
                    src, dst, self.send_sem.at[SLOTS[(e1, e2, kind)] * self.count + j],
                    self.recv_sem.at[(r1 * 4 + r2) * self.count + j],
                    dev(rem4(self.x + dx), rem4(self.y + dy), self.z, self.c),
                ).start()

            if e2 == 0:
                if e1 == 0:
                    send(0, True, 1, 1, 0)
                    send(1, True, -1, 3, 0)
                if e1 == 1:
                    send(0, True, 1, 2, 0)
                send(2, False, 1, e1, 1)
                send(3, False, -1, e1, 3)
            elif e2 == 1:
                send(2, False, 1, e1, 2)
            if extra is not None:
                extra(src, s, (e1 * 4 + e2) * 2 + j, 1 - 2 * j)
            return 0

        lax.fori_loop(0, self.count, body, 0)

    def drain(self):
        t = self.tiles(0)

        def body(i, _):
            remote(t, t, self.send_sem.at[i], self.recv_sem.at[0], (self.p, self.q)).wait_send()
            return 0

        lax.fori_loop(0, self.count * len(SLOTS), body, 0)


def plane_peers():
    p, q, x, y, z, c = place()
    return [
        dev(rem4(x + 1), y, z, c), dev(rem4(x - 1), y, z, c),
        dev(x, rem4(y + 1), z, c), dev(x, rem4(y - 1), z, c),
    ]


def relay_steps(plane, h_ref, zsem, psem, hsem):
    p, q, x, y, z, c = place()
    k = lax.rem(p, 8)
    zs, cs = k // 2, lax.rem(k, 2)
    here, partner = (p, q), dev(x, y, z, 1 - c)
    chain = c == cs
    source = jnp.logical_and(chain, z == zs)

    def feed(src, s, h, d):
        @pl.when(source)
        def _():
            remote(src, h_ref.at[s], zsem.at[h], hsem.at[h], dev(x, y, rem4(z + d), c)).start()
            remote(src, h_ref.at[s], psem.at[h], hsem.at[h], partner).start()

    def relay(e1, e2, r):
        def body(j, _):
            d = 1 - 2 * j
            h = (e1 * 4 + e2) * 2 + j

            @pl.when(jnp.logical_and(chain, rem4((z - zs) * d) == r))
            def _():
                t = h_ref.at[plane.tile(e1, e2, j)]
                remote(t, t, zsem.at[0], hsem.at[h], here).wait_recv()
                if r < 3:
                    remote(t, t, zsem.at[h], hsem.at[h], dev(x, y, rem4(z + d), c)).start()
                remote(t, t, psem.at[h], hsem.at[h], partner).start()

            return 0

        lax.fori_loop(0, 2, body, 0)

    def step(n):
        if n < len(COMBOS):
            plane.event(*COMBOS[n], extra=feed)
        for r in (1, 2, 3):
            if 0 <= n - 2 * r < len(COMBOS):
                relay(*COMBOS[n - 2 * r], r)

    def drain():
        t = h_ref.at[0]

        def last(i, _):
            d = 1 - 2 * lax.rem(i, 2)

            @pl.when(jnp.logical_and(chain, rem4((z - zs) * d) < 3))
            def _():
                remote(t, t, zsem.at[i], hsem.at[0], here).wait_send()

            @pl.when(chain)
            def _():
                remote(t, t, psem.at[i], hsem.at[0], here).wait_send()

            @pl.when(jnp.logical_not(chain))
            def _():
                remote(t, t, zsem.at[0], hsem.at[i], here).wait_recv()

            return 0

        lax.fori_loop(0, SCEN // 2, last, 0)

    return [lambda n=n: step(n) for n in range(len(COMBOS) + 6)], drain


PARTS = {
    (0, 0): [(0, 2)], (1, 0): [(0, 3), (1, 3)], (1, 1): [(1, 2)],
    (2, 0): [(0, 0), (2, 0)], (2, 1): [(0, 1), (3, 0)], (2, 2): [(2, 2)],
    (3, 0): [(1, 0), (2, 1)], (3, 1): [(1, 1), (3, 1)], (3, 2): [(2, 3), (3, 3)],
    (3, 3): [(3, 2)],
}


PACE = (1, 1, 1, 1, 1, 1, 1, 1)


def front_kernel(b_ref, bm_ref, bar_ref, g_ref, h_ref, w_ref,
                 xb, xc, part, rbuf, fin, zb, pk, v_ref,
                 loc, s1, r1, s2, r2, s3, r3, s4, r4, s5, r5,
                 ssem, rsem, zsem, psem, hsem):
    p, q, x, y, z, c = place()
    here, partner = (p, q), dev(x, y, z, 1 - c)
    greet([(lax.rem(p + i, 16), q) for i in range(1, 16)]
          + [(p, lax.rem(q + i, 8)) for i in range(1, 8)])
    own = pltpu.make_async_copy(b_ref, g_ref.at[pl.ds(2 * p, 2)], loc)
    own.start()
    plane = Plane(2, lambda j: b_ref.at[j], lambda s: g_ref.at[s], ssem, rsem)
    steps, drain = relay_steps(plane, h_ref, zsem, psem, hsem)

    def go(spot):
        for _ in range(min(len(steps), PACE[spot])):
            steps.pop(0)()

    go(0)
    holds = q < 4
    facing = dev(x, y, lax.rem(z + 1, 2), c)

    def to_partner():
        return remote(bm_ref, xb, s1.at[0], r1.at[0], partner)

    def to_facing():
        return remote(bm_ref.at[pl.ds(2 * lax.rem(z, 2), 2)], xc, s1.at[1], r1.at[1], facing)

    def slab(v):
        return v.reshape(v.shape[0] * TB, TB)

    def product(left, right):
        return lax.dot_general(slab(left), slab(right), TN, preferred_element_type=F32)

    def put(t, tile):
        part[:, t] = tile.reshape(16, 16, TB)

    def slices(i):
        g = lax.rem(p + i, 16)
        return remote(part.at[g], rbuf.at[p], s2.at[i - 1], r2.at[i - 1], (g, q))

    def halves(i):
        to = lax.rem(q + i, 8)
        return remote(fin.at[lax.rem(to, 2)], zb.at[q], s3.at[i - 1], r3.at[q], (p, to))

    @pl.when(holds)
    def _():
        to_facing().start()
        to_partner().start()
        put(2, product(bm_ref[...], bm_ref[...]))
        to_partner().wait_recv()

        def both(first, second):
            sl = pl.ds(2 * c, 2)
            put(3, product(second[sl], first[sl]))
            to_facing().wait_recv()

            @pl.when(z == 0)
            def _():
                put(0, product(xc[...], first[2:4]))
                put(1, product(xc[...], second[2:4]))

            @pl.when(z == 1)
            def _():
                put(0, product(first[0:2], xc[...]))
                put(1, product(second[0:2], xc[...]))

        @pl.when(c == 0)
        def _():
            both(bm_ref, xb)

        @pl.when(c == 1)
        def _():
            both(xb, bm_ref)

        for i in range(1, 16):
            slices(i).start()
        rbuf[p] = part[p]

    go(1)

    @pl.when(holds)
    def _():
        for i in range(1, 16):
            t = rbuf.at[lax.rem(p + 16 - i, 16)]
            remote(t, t, s2.at[i - 1], r2.at[i - 1], here).wait_recv()
        total = rbuf[0]
        for i in range(1, 16):
            total = total + rbuf[i]
        fin[0] = total[:, 0:8]
        fin[1] = total[:, 8:16]
        for i in range(1, 8):
            halves(i).start()
        zb[lax.rem(q, 4)] = fin[c]

    go(2)
    for m in range(4):
        @pl.when(q != m)
        def _():
            remote(zb.at[m], zb.at[m], s3.at[0], r3.at[m], here).wait_recv()

    at = (lax.broadcasted_iota(jnp.int32, (8, TB), 1)
          == p * 16 + c * 8 + lax.broadcasted_iota(jnp.int32, (8, TB), 0))
    for (k, m), parts in PARTS.items():
        v = zb[parts[0][0], parts[0][1]]
        for owner, t in parts[1:]:
            v = v + zb[owner, t]
        if k == m:
            v = v + jnp.where(at, bar_ref[k:k + 1, :], 0.0)
        first = (k * (k + 1) // 2 + m) * TB
        pk[p, c, :, first:first + TB] = v

    def shard(i):
        return remote(pk.at[p, c], pk.at[p, c], s4.at[i - 1], r4.at[i - 1],
                      (lax.rem(p + i, 16), q))

    def pass_on(i):
        t = pk.at[lax.rem(p + 16 - i, 16), c]
        return remote(t, t, s5.at[i], r5.at[i], partner)

    for i in range(1, 16):
        shard(i).start()
    pass_on(0).start()
    go(3)
    for i in range(1, 16):
        t = pk.at[lax.rem(p + 16 - i, 16), c]
        remote(t, t, s4.at[i - 1], r4.at[i - 1], here).wait_recv()
        pass_on(i).start()
        if i % 5 == 0:
            go(3 + i // 5)
    for i in range(16):
        t = pk.at[lax.rem(p + 16 - i, 16), 1 - c]
        remote(t, t, s5.at[i], r5.at[i], here).wait_recv()

    for k in range(4):
        width = TB * (k + 1)
        first = TB * (k * (k + 1) // 2)
        w_ref[TB * k:TB * (k + 1), 0:width] = pk[:, :, :, first:first + width].reshape(TB, width)
    blocks = PW // NB

    for n in range(blocks):
        lo, hi = NB * n, NB * (n + 1)
        turned = invert_factor(w_ref[lo:hi, lo:hi]).T
        go(7)
        v = jnp.dot(left_parts(w_ref[:, lo:hi]), right_parts(turned, 0),
                    preferred_element_type=F32)
        w_ref[:, lo:hi] = v
        w_ref[lo:hi, lo:hi] = turned
        if hi < PW:
            v_ref[...] = left_parts(w_ref[:, lo:hi])
            below = right_parts(w_ref[hi:PW, lo:hi], 1)
            w_ref[lo:hi, hi:PW] = jnp.zeros((NB, PW - hi), F32)
            for jl in range(hi, PW, TB):
                jh = min(jl + TB, PW)
                w_ref[:, jl:jh] -= lax.dot_general(
                    v_ref[...], below[jl - hi:jh - hi], NT, preferred_element_type=F32)
        go(7)
    while steps:
        steps.pop(0)()

    own.wait()
    plane.drain()
    drain()

    @pl.when(holds)
    def _():
        to_partner().wait_send()
        to_facing().wait_send()
        for i in range(1, 16):
            slices(i).wait_send()
        for i in range(1, 8):
            halves(i).wait_send()

    for i in range(1, 16):
        shard(i).wait_send()
    for i in range(16):
        pass_on(i).wait_send()


def front(border, masked, barrier):
    tiles = jax.ShapeDtypeStruct((SCEN // 2, 2, TB, TB), BF16)
    hbm = pl.BlockSpec(memory_space=pl.ANY)
    vmem = pl.BlockSpec(memory_space=pltpu.VMEM)
    return pl.pallas_call(
        front_kernel,
        out_shape=(tiles, tiles, jax.ShapeDtypeStruct((PW, PW), F32)),
        in_specs=[hbm, vmem, vmem],
        out_specs=(hbm, hbm, vmem),
        scratch_shapes=[
            pltpu.VMEM((4, TB, TB), BF16), pltpu.VMEM((2, TB, TB), BF16),
            pltpu.VMEM((16, 4, 16, TB), F32), pltpu.VMEM((16, 4, 16, TB), F32),
            pltpu.VMEM((2, 4, 8, TB), F32), pltpu.VMEM((4, 4, 8, TB), F32),
            pltpu.VMEM((16, 2, 8, 2560), F32), pltpu.VMEM((PW, 6 * NB), BF16),
            DMA(()), DMA((2,)), DMA((2,)), DMA((15,)), DMA((15,)), DMA((7,)), DMA((4,)),
            DMA((15,)), DMA((15,)), DMA((16,)), DMA((16,)),
            DMA((30,)), DMA((32,)), DMA((32,)), DMA((32,)), DMA((32,)),
        ],
        compiler_params=pltpu.CompilerParams(
            collective_id=0, has_side_effects=True, vmem_limit_bytes=48 * MIB),
        name="front",
    )(border.reshape(2, 2, TB, TB), masked, barrier)


PER_STEP = 4


def schur_kernel(touched_ref, list_ref, count_ref, *refs):
    g_refs, h_refs = refs[:PER_STEP], refs[PER_STEP:2 * PER_STEP]
    bar_ref, out_ref, prod_ref = refs[2 * PER_STEP:]
    p, q = lax.axis_index("scen"), lax.axis_index("col")
    k = lax.rem(p, 8)
    step = pl.program_id(0)
    diagonal = k == q

    @pl.when(step == 0)
    def _():
        out_ref[...] = jnp.zeros_like(out_ref)

        @pl.when(diagonal)
        def _():
            eye = lax.broadcasted_iota(jnp.int32, (TB, TB), 0) == lax.broadcasted_iota(
                jnp.int32, (TB, TB), 1
            )
            for a in range(4):
                col = lane((2 * a + p // 8) * TB)
                row = bar_ref[pl.ds(a * 16 + p, 1), :]
                out_ref[a * TB:(a + 1) * TB, pl.ds(col, TB)] = jnp.where(eye, row, 0.0)

    @pl.when(step * PER_STEP < count_ref[0])
    def _():
        for i in range(PER_STEP):
            right = g_refs[i][0]
            left = jnp.where(diagonal, right, h_refs[i][0])
            prod_ref[i] = lax.dot_general(left, right, TN, preferred_element_type=F32)

        for i in range(PER_STEP):
            @pl.when(step * PER_STEP + i < count_ref[0])
            def _():
                s = list_ref[step * PER_STEP + i]
                row = pl.multiple_of((touched_ref[s, k] // 16) * TB, TB)
                col = lane((touched_ref[s, q] // 8) * TB)
                out_ref[pl.ds(row, TB), pl.ds(col, TB)] += prod_ref[i]


def assemble(touched, gathered, rows, barrier):
    p = lax.axis_index("scen")
    index = jnp.arange(SCEN, dtype=jnp.int32)
    mine = lax.dynamic_index_in_dim(touched, lax.rem(p, 8), 1, keepdims=False) % 16 == p
    place_of = jnp.sum(jnp.where(mine[None, :] & (index[None, :] < index[:, None]), 1, 0), axis=1)
    listed = jnp.sum(
        jnp.where(mine[None, :] & (place_of[None, :] == index[:, None]), index[None, :], 0), axis=1)
    count = jnp.sum(mine.astype(jnp.int32)).reshape(1)
    blocks = [
        pl.BlockSpec((1, TB, TB), lambda i, t, l, c, j=j: (l[i * PER_STEP + j], 0, 0))
        for j in range(PER_STEP)
    ]
    return pl.pallas_call(
        schur_kernel,
        out_shape=jax.ShapeDtypeStruct((1024, 2048), F32),
        grid_spec=pltpu.PrefetchScalarGridSpec(
            num_scalar_prefetch=3,
            grid=(SCEN // PER_STEP,),
            in_specs=blocks + blocks + [pl.BlockSpec((N // TB, TB), lambda i, t, l, c: (0, 0))],
            out_specs=pl.BlockSpec((1024, 2048), lambda i, t, l, c: (0, 0)),
            scratch_shapes=[pltpu.VMEM((PER_STEP, TB, TB), F32)],
        ),
        compiler_params=pltpu.CompilerParams(vmem_limit_bytes=60 * MIB),
        name="assemble",
    )(touched, listed, count, *[gathered.reshape(SCEN, TB, TB)] * PER_STEP,
      *[rows.reshape(SCEN, TB, TB)] * PER_STEP, barrier)


def pivot_pair(a, b, d):
    q0 = lax.rsqrt(a)
    q1 = lax.rsqrt(a * (a * d - b * b))
    inv = q1 * q1 * a
    return q0, q1, d * inv, b * inv, a * inv


def pivot_four(w):
    (w00,), (w10, w11), (w20, w21, w22), (w30, w31, w32, w33) = w
    q0, q1, ci, bi, ai = pivot_pair(w00, w10, w11)
    e02, e12 = ci * w20 - bi * w21, ai * w21 - bi * w20
    e03, e13 = ci * w30 - bi * w31, ai * w31 - bi * w30
    v22 = w22 - w20 * e02 - w21 * e12
    v32 = w32 - w30 * e02 - w31 * e12
    v33 = w33 - w30 * e03 - w31 * e13
    q2, q3, cj, bj, aj = pivot_pair(v22, v32, v33)

    def solve(r0, r1, r2, r3):
        z0, z1 = ci * r0 - bi * r1, ai * r1 - bi * r0
        s2, s3 = r2 - w20 * z0 - w21 * z1, r3 - w30 * z0 - w31 * z1
        z2, z3 = cj * s2 - bj * s3, aj * s3 - bj * s2
        return z0 - e02 * z2 - e03 * z3, z1 - e12 * z2 - e13 * z3, z2, z3, s2, s3

    def half(r0, r1, s2, s3):
        return [r0 * q0, (w00 * r1 - w10 * r0) * q1, s2 * q2, (v22 * s3 - v32 * s2) * q3]

    return solve, half


def splat(row, at):
    return jnp.broadcast_to(row[:, at:at + 1], (1, NB))


HB = NB // 2


def small_inverse(a):
    eye = (
        lax.broadcasted_iota(jnp.int32, (HB, HB), 0)
        == lax.broadcasted_iota(jnp.int32, (HB, HB), 1)
    ).astype(F32)
    t = jnp.concatenate([a, eye], axis=1)
    top, rows, w = 0, [], None
    for o in range(0, HB, 4):
        if 8 * (o // 8) > top:
            t, top = t[8 * (o // 8) - top:], 8 * (o // 8)
        k, height = o - top, t.shape[0]
        c = [jnp.broadcast_to(t[:, o + i:o + i + 1], (height, NB)) for i in range(4)]
        r = [t[k + i:k + i + 1, :] for i in range(4)]
        if w is None:
            w = [[c[v][k + u:k + u + 1, :] for v in range(u + 1)] for u in range(4)]
        solve, half = pivot_four(w)
        last = o + 4 == HB
        if not last:
            after = [t[k + 4 + i:k + 5 + i, :] for i in range(4)]
            g = [[splat(r[i], o + 4 + u) for u in range(4)] for i in range(4)]
            z = [solve(*[g[i][v] for i in range(4)]) for v in range(4)]
            w = [[splat(after[u], o + 4 + v)
                  - (g[0][u] * z[v][0] + g[1][u] * z[v][1])
                  - (g[2][u] * z[v][2] + g[3][u] * z[v][3]) for v in range(u + 1)]
                 for u in range(4)]
        z0, z1, z2, z3, s2, s3 = solve(*r)
        rows += half(r[0], r[1], s2, s3)
        if not last:
            t = t - (c[0] * z0 + c[1] * z1) - (c[2] * z2 + c[3] * z3)
    return jnp.concatenate(rows, 0)[:, HB:NB]


def wide(a, b, dims=(((1,), (0,)), ((), ()))):
    return lax.dot_general(a, b, dims, precision=HIGHEST, preferred_element_type=F32)


def thirds(v):
    a = v.astype(BF16)
    rest = v - a.astype(F32)
    b = rest.astype(BF16)
    return a, b, (rest - b.astype(F32)).astype(BF16)


def left_parts(v):
    a, b, c = thirds(v)
    return jnp.concatenate([a, a, b, b, a, c], axis=1)


def right_parts(v, axis):
    a, b, c = thirds(v)
    return jnp.concatenate([a, b, a, b, c, a], axis=axis)


def invert_factor(a):
    x1 = small_inverse(a[:HB, :HB])
    l = wide(a[HB:, :HB], x1, NT)
    x2 = small_inverse(a[HB:, HB:] - wide(l, l, NT))
    x21 = -wide(wide(x2, l), x1)
    return jnp.concatenate([
        jnp.concatenate([x1, jnp.zeros((HB, HB), F32)], 1),
        jnp.concatenate([x21, x2], 1)], 0)


def panel_kernel(s_ref, w_hbm, pc_ref, pr_ref, pan_ref, w_ref, raw_ref, pf_ref, pb_ref,
                 loc, asend, arecv, wsend, wrecv, ssem, rsem,
                 zsend, zrecv, csend, crecv, fsend, frecv):
    p, q, x, y, z, c = place()
    here, partner = (p, q), dev(x, y, z, 1 - c)
    twin = (8 * (p // 8) + q, lax.rem(p, 8))
    alone = lax.rem(p, 8) == q
    bar = pltpu.get_barrier_semaphore()
    for d in plane_peers() + [(p, lax.rem(q + i, 8)) for i in range(1, 8)]:
        pl.semaphore_signal(bar, inc=1, device_id=d, device_id_type=MESH)

    @pl.when(alone)
    def _():
        pl.semaphore_wait(bar, 11)

    @pl.when(jnp.logical_not(alone))
    def _():
        pl.semaphore_signal(bar, inc=1, device_id=twin, device_id_type=MESH)
        pl.semaphore_wait(bar, 12)

    holds = q < 4
    mine = lane(lax.rem(q, 4) * TB)

    def rows_to(i):
        to = lax.rem(q + i, 8)
        return remote(s_ref.at[pl.ds(16 * to, 16), :, pl.ds(0, TB)],
                      raw_ref.at[:, :, pl.ds(mine, TB)],
                      asend.at[i - 1], arecv.at[lax.rem(q, 4)], (p, to))

    own_rows = pltpu.make_async_copy(
        s_ref.at[pl.ds(16 * q, 16), :, pl.ds(0, TB)], raw_ref.at[:, :, pl.ds(mine, TB)], loc.at[0])
    inverse = pltpu.make_async_copy(w_hbm, w_ref, loc.at[1])

    @pl.when(holds)
    def _():
        for i in (2, 3, 4, 5, 6, 1, 7):
            rows_to(i).start()
        own_rows.start()

    inverse.start()
    for m in range(4):
        @pl.when(q == m)
        def _():
            own_rows.wait()

        @pl.when(q != m)
        def _():
            t = raw_ref.at[:, :, pl.ds(m * TB, TB)]
            remote(t, t, asend.at[0], arecv.at[m], here).wait_recv()

    inverse.wait()
    for n in range(PW // NB):
        lo, hi = NB * n, NB * (n + 1)
        v = jnp.dot(raw_ref[:, :, 0:hi].reshape(NB, hi), w_ref[0:hi, lo:hi],
                    precision=HIGHEST, preferred_element_type=F32)
        pf_ref[:, :, lo:hi] = v.reshape(16, 8, NB)
        pb_ref[:, :, lo:hi] = v.astype(BF16).reshape(4, 32, NB)

    def to_twin():
        return remote(pb_ref, pc_ref.at[twin[0]], wsend, wrecv, twin)

    keep_cols = pltpu.make_async_copy(pb_ref, pc_ref.at[p], loc.at[2])
    keep_rows = pltpu.make_async_copy(pb_ref, pr_ref.at[q], loc.at[3])

    @pl.when(alone)
    def _():
        keep_cols.start()

    @pl.when(jnp.logical_not(alone))
    def _():
        to_twin().start()

    keep_rows.start()

    def over(i):
        return remote(pb_ref, pr_ref.at[q], zsend.at[i - 1], zrecv.at[i - 1],
                      dev(x, y, rem4(z + i), c))

    def across(i):
        src = pb_ref if i == 0 else pr_ref.at[2 * rem4(z - i) + c]
        return remote(src, pr_ref.at[2 * rem4(z - i) + c], csend.at[i], crecv.at[i], partner)

    def block(m):
        return remote(pf_ref.at[:, :, pl.ds(m * TB, TB)], pan_ref.at[q],
                      fsend.at[m], frecv.at[q], (p, m))

    def block_here(m):
        return pltpu.make_async_copy(
            pf_ref.at[:, :, pl.ds(m * TB, TB)], pan_ref.at[q], loc.at[4])

    plane = Plane(
        4, lambda j: pc_ref.at[p, j], lambda s: pc_ref.at[s // 4, lax.rem(s, 4)], ssem, rsem)

    @pl.when(alone)
    def _():
        keep_cols.wait()

    @pl.when(jnp.logical_not(alone))
    def _():
        remote(pb_ref, pc_ref.at[p], wsend, wrecv, twin).wait_recv()

    for n in range(len(COMBOS)):
        plane.event(*COMBOS[n])
        if n == 0:
            for i in (1, 3, 2):
                over(i).start()
            across(0).start()
            for m in range(4):
                @pl.when(q != m)
                def _():
                    block(m).start()

                @pl.when(q == m)
                def _():
                    block_here(m).start()
        if n in (4, 6, 8):
            i = {4: 1, 6: 3, 8: 2}[n]
            t = pr_ref.at[2 * rem4(z - i) + c]
            remote(t, t, zsend.at[0], zrecv.at[i - 1], here).wait_recv()
            across(i).start()
    plane.drain()
    keep_rows.wait()
    for i in (1, 2, 3):
        over(i).wait_send()
    for i in range(4):
        across(i).wait_send()
        t = pr_ref.at[2 * rem4(z - i) + 1 - c]
        remote(t, t, csend.at[0], crecv.at[i], here).wait_recv()
    for m in range(4):
        @pl.when(q != m)
        def _():
            block(m).wait_send()

        @pl.when(q == m)
        def _():
            block_here(m).wait()
            for i in range(1, 8):
                t = pan_ref.at[lax.rem(q + i, 8)]
                remote(t, t, fsend.at[0], frecv.at[lax.rem(q + i, 8)], here).wait_recv()

    @pl.when(jnp.logical_not(alone))
    def _():
        to_twin().wait_send()

    @pl.when(holds)
    def _():
        for i in range(1, 8):
            rows_to(i).wait_send()


def solve_panel(schur, inverse):
    hbm = pl.BlockSpec(memory_space=pl.ANY)
    return pl.pallas_call(
        panel_kernel,
        out_shape=(
            jax.ShapeDtypeStruct((16, 4, 32, PW), BF16),
            jax.ShapeDtypeStruct((8, 4, 32, PW), BF16),
            jax.ShapeDtypeStruct((8, 16, 8, TB), F32),
        ),
        in_specs=[hbm, hbm],
        out_specs=(hbm, hbm, hbm),
        scratch_shapes=[
            pltpu.VMEM((PW, PW), F32), pltpu.VMEM((16, 8, PW), F32),
            pltpu.VMEM((16, 8, PW), F32), pltpu.VMEM((4, 32, PW), BF16),
            DMA((5,)), DMA((7,)), DMA((4,)), DMA(()), DMA(()), DMA((60,)), DMA((64,)),
            DMA((3,)), DMA((3,)), DMA((4,)), DMA((4,)), DMA((4,)), DMA((8,)),
        ],
        compiler_params=pltpu.CompilerParams(
            collective_id=1, has_side_effects=True, vmem_limit_bytes=32 * MIB),
        name="solve_panel",
    )(schur.reshape(128, 8, 2048), inverse)


STRIP = 256


def update_kernel(s_ref, pr_ref, pc_ref, pan_ref, out_ref):
    p, q = lax.axis_index("scen"), lax.axis_index("col")
    a = pl.program_id(0) // (TB // STRIP)
    low = jnp.logical_or(a > 0, p >= 4)
    panel = q < 4
    for b in range(8):
        cols = slice(b * TB, (b + 1) * TB)
        first = (b % 2) * 1024 + (b // 2) * TB

        def lowered():
            out_ref[:, cols] = s_ref[:, cols] - lax.dot_general(
                pr_ref[...], pc_ref[first:first + TB, :], NT, preferred_element_type=F32)

        def kept():
            out_ref[:, cols] = s_ref[:, cols]

        def solved():
            out_ref[:, cols] = pan_ref[...]

        if b == 0:
            pl.when(panel)(solved)
            pl.when(jnp.logical_and(jnp.logical_not(panel), low))(lowered)
            pl.when(jnp.logical_and(jnp.logical_not(panel), jnp.logical_not(low)))(kept)
        else:
            pl.when(low)(lowered)
            pl.when(jnp.logical_not(low))(kept)


def update(schur, rows, cols, panel):
    strip = pl.BlockSpec((STRIP, 2048), lambda i: (i, 0))
    return pl.pallas_call(
        update_kernel,
        out_shape=jax.ShapeDtypeStruct((1024, 2048), F32),
        grid=(1024 // STRIP,),
        in_specs=[
            strip,
            pl.BlockSpec((STRIP, PW), lambda i: (i, 0)),
            pl.BlockSpec((2048, PW), lambda i: (0, 0)),
            pl.BlockSpec((STRIP, TB), lambda i: (i, 0)),
        ],
        out_specs=strip,
        compiler_params=pltpu.CompilerParams(vmem_limit_bytes=48 * MIB),
        name="update",
    )(schur, rows.reshape(1024, PW), cols.reshape(2048, PW), panel.reshape(1024, TB))


def per_device(border, touched, barrier):
    p, q = lax.axis_index("scen"), lax.axis_index("col")
    mine = lax.dynamic_slice(touched, (4 * p, q), (4, 1))
    masked = jnp.where((mine == q)[:, :, None], border, jnp.zeros_like(border))
    barrier = barrier.reshape(N // TB, TB)
    gathered, rows, inverse = front(border, masked, barrier)
    schur = assemble(touched, gathered, rows, barrier)
    panel_cols, panel_rows, panel = solve_panel(schur, inverse)
    return update(schur, panel_rows, panel_cols, panel)


def solution(mesh):
    in_specs = (P("scen", None, "col"), P(), P())
    out_specs = P("scen", "col")
    return jax.shard_map(
        per_device, mesh=mesh, in_specs=in_specs, out_specs=out_specs, check_vma=False
    )
```

```python
import jax
import jax.numpy as jnp
from jax import lax
from jax.experimental import pallas as pl
from jax.experimental.pallas import tpu as pltpu
from jax.sharding import PartitionSpec as P

N = 16384
TB = 256
KT = 8
PW = 1024
SCEN = 64
NB = 128
F32 = jnp.float32
BF16 = jnp.bfloat16
HIGHEST = lax.Precision.HIGHEST
MESH = pl.DeviceIdType.MESH
DMA = pltpu.SemaphoreType.DMA
NT = (((1,), (1,)), ((), ()))
TN = (((0,), (0,)), ((), ()))
MIB = 1024 * 1024

COMBOS = [
    (0, 0), (1, 0), (3, 0), (0, 1), (0, 3), (2, 0), (0, 2), (1, 1),
    (1, 3), (3, 1), (3, 3), (2, 1), (2, 3), (1, 2), (3, 2), (2, 2),
]


def plane_slots():
    slots = {}
    for e1, e2 in COMBOS:
        if e2 == 0:
            kinds = {0: (0, 1, 2, 3), 1: (0, 2, 3)}.get(e1, (2, 3))
        else:
            kinds = (2,) if e2 == 1 else ()
        for kind in kinds:
            slots[(e1, e2, kind)] = len(slots)
    return slots


SLOTS = plane_slots()


def rem4(v):
    return lax.rem(v + 8, 4)


def place():
    p = lax.axis_index("scen")
    q = lax.axis_index("col")
    return p, q, p // 4, lax.rem(p, 4), q // 2, lax.rem(q, 2)


def dev(x, y, z, c):
    return (x * 4 + y, z * 2 + c)


def remote(src, dst, send, recv, device):
    return pltpu.make_async_remote_copy(
        src_ref=src, dst_ref=dst, send_sem=send, recv_sem=recv,
        device_id=device, device_id_type=MESH,
    )


def greet(devices):
    bar = pltpu.get_barrier_semaphore()
    for d in devices:
        pl.semaphore_signal(bar, inc=1, device_id=d, device_id_type=MESH)
    pl.semaphore_wait(bar, len(devices))


def lane(v):
    return pl.multiple_of(v, 128)


class Plane:
    def __init__(self, count, own, tiles, send_sem, recv_sem):
        self.count = count
        self.own, self.tiles = own, tiles
        self.send_sem, self.recv_sem = send_sem, recv_sem
        self.p, self.q, self.x, self.y, self.z, self.c = place()

    def geom(self, j):
        if self.count == 2:
            return 1 - j, j, 1, -1
        sy = j // 2
        d = 1 - 2 * lax.rem(j, 2)
        return 1 - sy, sy, d, d

    def tile(self, e1, e2, j):
        sx, sy, d1, d2 = self.geom(j)
        ox = rem4(self.x - d1 * e1 * sx - d2 * e2 * sy)
        oy = rem4(self.y - d1 * e1 * sy - d2 * e2 * sx)
        return self.count * (ox * 4 + oy) + j

    def event(self, e1, e2, extra=None):
        def body(j, _):
            sx, sy, d1, d2 = self.geom(j)
            s = self.tile(e1, e2, j)
            dst = self.tiles(s)
            if (e1, e2) == (0, 0):
                src = self.own(j)
            else:
                src = dst
                remote(
                    src, src, self.send_sem.at[0],
                    self.recv_sem.at[(e1 * 4 + e2) * self.count + j], (self.p, self.q),
                ).wait_recv()

            def send(kind, first, sign, r1, r2):
                dx = sx * d1 * sign if first else sy * d2 * sign
                dy = sy * d1 * sign if first else sx * d2 * sign
                remote(
                    src, dst, self.send_sem.at[SLOTS[(e1, e2, kind)] * self.count + j],
                    self.recv_sem.at[(r1 * 4 + r2) * self.count + j],
                    dev(rem4(self.x + dx), rem4(self.y + dy), self.z, self.c),
                ).start()

            if e2 == 0:
                if e1 == 0:
                    send(0, True, 1, 1, 0)
                    send(1, True, -1, 3, 0)
                if e1 == 1:
                    send(0, True, 1, 2, 0)
                send(2, False, 1, e1, 1)
                send(3, False, -1, e1, 3)
            elif e2 == 1:
                send(2, False, 1, e1, 2)
            if extra is not None:
                extra(src, s, (e1 * 4 + e2) * 2 + j, 1 - 2 * j)
            return 0

        lax.fori_loop(0, self.count, body, 0)

    def drain(self):
        t = self.tiles(0)

        def body(i, _):
            remote(t, t, self.send_sem.at[i], self.recv_sem.at[0], (self.p, self.q)).wait_send()
            return 0

        lax.fori_loop(0, self.count * len(SLOTS), body, 0)


def plane_peers():
    p, q, x, y, z, c = place()
    return [
        dev(rem4(x + 1), y, z, c), dev(rem4(x - 1), y, z, c),
        dev(x, rem4(y + 1), z, c), dev(x, rem4(y - 1), z, c),
    ]


def relay_steps(plane, h_ref, zsem, psem, hsem):
    p, q, x, y, z, c = place()
    k = lax.rem(p, 8)
    zs, cs = k // 2, lax.rem(k, 2)
    here, partner = (p, q), dev(x, y, z, 1 - c)
    chain = c == cs
    source = jnp.logical_and(chain, z == zs)

    def feed(src, s, h, d):
        @pl.when(source)
        def _():
            remote(src, h_ref.at[s], zsem.at[h], hsem.at[h], dev(x, y, rem4(z + d), c)).start()
            remote(src, h_ref.at[s], psem.at[h], hsem.at[h], partner).start()

    def relay(e1, e2, r):
        def body(j, _):
            d = 1 - 2 * j
            h = (e1 * 4 + e2) * 2 + j

            @pl.when(jnp.logical_and(chain, rem4((z - zs) * d) == r))
            def _():
                t = h_ref.at[plane.tile(e1, e2, j)]
                remote(t, t, zsem.at[0], hsem.at[h], here).wait_recv()
                if r < 3:
                    remote(t, t, zsem.at[h], hsem.at[h], dev(x, y, rem4(z + d), c)).start()
                remote(t, t, psem.at[h], hsem.at[h], partner).start()

            return 0

        lax.fori_loop(0, 2, body, 0)

    def step(n):
        if n < len(COMBOS):
            plane.event(*COMBOS[n], extra=feed)
        for r in (1, 2, 3):
            if 0 <= n - 2 * r < len(COMBOS):
                relay(*COMBOS[n - 2 * r], r)

    def drain():
        t = h_ref.at[0]

        def last(i, _):
            d = 1 - 2 * lax.rem(i, 2)

            @pl.when(jnp.logical_and(chain, rem4((z - zs) * d) < 3))
            def _():
                remote(t, t, zsem.at[i], hsem.at[0], here).wait_send()

            @pl.when(chain)
            def _():
                remote(t, t, psem.at[i], hsem.at[0], here).wait_send()

            @pl.when(jnp.logical_not(chain))
            def _():
                remote(t, t, zsem.at[0], hsem.at[i], here).wait_recv()

            return 0

        lax.fori_loop(0, SCEN // 2, last, 0)

    return [lambda n=n: step(n) for n in range(len(COMBOS) + 6)], drain


PARTS = {
    (0, 0): [(0, 2)], (1, 0): [(0, 3), (1, 3)], (1, 1): [(1, 2)],
    (2, 0): [(0, 0), (2, 0)], (2, 1): [(0, 1), (3, 0)], (2, 2): [(2, 2)],
    (3, 0): [(1, 0), (2, 1)], (3, 1): [(1, 1), (3, 1)], (3, 2): [(2, 3), (3, 3)],
    (3, 3): [(3, 2)],
}


PACE = (1, 1, 1, 1, 1, 1, 1, 1)


def front_kernel(b_ref, bm_ref, bar_ref, g_ref, h_ref, w_out,
                 xb, xc, part, rbuf, fin, zb, pk, v_ref, w_ref,
                 loc, wloc, s1, r1, s2, r2, s3, r3, s4, r4, s5, r5,
                 ssem, rsem, zsem, psem, hsem):
    p, q, x, y, z, c = place()
    here, partner = (p, q), dev(x, y, z, 1 - c)
    greet([(lax.rem(p + i, 16), q) for i in range(1, 16)]
          + [(p, lax.rem(q + i, 8)) for i in range(1, 8)])
    own = pltpu.make_async_copy(b_ref, g_ref.at[pl.ds(2 * p, 2)], loc)
    own.start()
    plane = Plane(2, lambda j: b_ref.at[j], lambda s: g_ref.at[s], ssem, rsem)
    steps, drain = relay_steps(plane, h_ref, zsem, psem, hsem)

    def go(spot):
        for _ in range(min(len(steps), PACE[spot])):
            steps.pop(0)()

    go(0)
    holds = q < 4
    facing = dev(x, y, lax.rem(z + 1, 2), c)

    def to_partner():
        return remote(bm_ref, xb, s1.at[0], r1.at[0], partner)

    def to_facing():
        return remote(bm_ref.at[pl.ds(2 * lax.rem(z, 2), 2)], xc, s1.at[1], r1.at[1], facing)

    def slab(v):
        return v.reshape(v.shape[0] * TB, TB)

    def product(left, right):
        return lax.dot_general(slab(left), slab(right), TN, preferred_element_type=F32)

    def put(t, tile):
        part[:, t] = tile.reshape(16, 16, TB)

    def slices(i):
        g = lax.rem(p + i, 16)
        return remote(part.at[g], rbuf.at[p], s2.at[i - 1], r2.at[i - 1], (g, q))

    def halves(i):
        to = lax.rem(q + i, 8)
        return remote(fin.at[lax.rem(to, 2)], zb.at[q], s3.at[i - 1], r3.at[q], (p, to))

    @pl.when(holds)
    def _():
        to_facing().start()
        to_partner().start()
        put(2, product(bm_ref[...], bm_ref[...]))
        to_partner().wait_recv()

        def both(first, second):
            sl = pl.ds(2 * c, 2)
            put(3, product(second[sl], first[sl]))
            to_facing().wait_recv()

            @pl.when(z == 0)
            def _():
                put(0, product(xc[...], first[2:4]))
                put(1, product(xc[...], second[2:4]))

            @pl.when(z == 1)
            def _():
                put(0, product(first[0:2], xc[...]))
                put(1, product(second[0:2], xc[...]))

        @pl.when(c == 0)
        def _():
            both(bm_ref, xb)

        @pl.when(c == 1)
        def _():
            both(xb, bm_ref)

        for i in range(1, 16):
            slices(i).start()
        rbuf[p] = part[p]

    go(1)

    @pl.when(holds)
    def _():
        for i in range(1, 16):
            t = rbuf.at[lax.rem(p + 16 - i, 16)]
            remote(t, t, s2.at[i - 1], r2.at[i - 1], here).wait_recv()
        total = rbuf[0]
        for i in range(1, 16):
            total = total + rbuf[i]
        fin[0] = total[:, 0:8]
        fin[1] = total[:, 8:16]
        for i in range(1, 8):
            halves(i).start()
        zb[lax.rem(q, 4)] = fin[c]

    go(2)
    for m in range(4):
        @pl.when(q != m)
        def _():
            remote(zb.at[m], zb.at[m], s3.at[0], r3.at[m], here).wait_recv()

    at = (lax.broadcasted_iota(jnp.int32, (8, TB), 1)
          == p * 16 + c * 8 + lax.broadcasted_iota(jnp.int32, (8, TB), 0))
    for (k, m), parts in PARTS.items():
        v = zb[parts[0][0], parts[0][1]]
        for owner, t in parts[1:]:
            v = v + zb[owner, t]
        if k == m:
            v = v + jnp.where(at, bar_ref[k:k + 1, :], 0.0)
        first = (k * (k + 1) // 2 + m) * TB
        pk[p, c, :, first:first + TB] = v

    def shard(i):
        return remote(pk.at[p, c], pk.at[p, c], s4.at[i - 1], r4.at[i - 1],
                      (lax.rem(p + i, 16), q))

    def pass_on(i):
        t = pk.at[lax.rem(p + 16 - i, 16), c]
        return remote(t, t, s5.at[i], r5.at[i], partner)

    for i in range(1, 16):
        shard(i).start()
    pass_on(0).start()
    go(3)
    for i in range(1, 16):
        t = pk.at[lax.rem(p + 16 - i, 16), c]
        remote(t, t, s4.at[i - 1], r4.at[i - 1], here).wait_recv()
        pass_on(i).start()
        if i % 5 == 0:
            go(3 + i // 5)
    for i in range(16):
        t = pk.at[lax.rem(p + 16 - i, 16), 1 - c]
        remote(t, t, s5.at[i], r5.at[i], here).wait_recv()

    for k in range(4):
        width = TB * (k + 1)
        first = TB * (k * (k + 1) // 2)
        w_ref[TB * k:TB * (k + 1), 0:width] = pk[:, :, :, first:first + width].reshape(TB, width)
    blocks = PW // NB

    for n in range(blocks):
        lo, hi = NB * n, NB * (n + 1)
        turned = invert_factor(w_ref[lo:hi, lo:hi]).T
        go(7)
        v = jnp.dot(left_parts(w_ref[:, lo:hi]), right_parts(turned, 0),
                    preferred_element_type=F32)
        w_ref[:, lo:hi] = v
        w_ref[lo:hi, lo:hi] = turned
        if hi < PW:
            v_ref[...] = left_parts(w_ref[:, lo:hi])
            below = right_parts(w_ref[hi:PW, lo:hi], 1)
            w_ref[lo:hi, hi:PW] = jnp.zeros((NB, PW - hi), F32)
            for jl in range(hi, PW, TB):
                jh = min(jl + TB, PW)
                w_ref[:, jl:jh] -= lax.dot_general(
                    v_ref[...], below[jl - hi:jh - hi], NT, preferred_element_type=F32)
        go(7)
    keep = pltpu.make_async_copy(w_ref, w_out, wloc)
    keep.start()
    while steps:
        steps.pop(0)()

    own.wait()
    keep.wait()
    plane.drain()
    drain()

    @pl.when(holds)
    def _():
        to_partner().wait_send()
        to_facing().wait_send()
        for i in range(1, 16):
            slices(i).wait_send()
        for i in range(1, 8):
            halves(i).wait_send()

    for i in range(1, 16):
        shard(i).wait_send()
    for i in range(16):
        pass_on(i).wait_send()


def front(border, masked, barrier):
    tiles = jax.ShapeDtypeStruct((SCEN // 2, 2, TB, TB), BF16)
    hbm = pl.BlockSpec(memory_space=pl.ANY)
    vmem = pl.BlockSpec(memory_space=pltpu.VMEM)
    return pl.pallas_call(
        front_kernel,
        out_shape=(tiles, tiles, jax.ShapeDtypeStruct((PW, PW), F32)),
        in_specs=[hbm, vmem, vmem],
        out_specs=(hbm, hbm, hbm),
        scratch_shapes=[
            pltpu.VMEM((4, TB, TB), BF16), pltpu.VMEM((2, TB, TB), BF16),
            pltpu.VMEM((16, 4, 16, TB), F32), pltpu.VMEM((16, 4, 16, TB), F32),
            pltpu.VMEM((2, 4, 8, TB), F32), pltpu.VMEM((4, 4, 8, TB), F32),
            pltpu.VMEM((16, 2, 8, 2560), F32), pltpu.VMEM((PW, 6 * NB), BF16),
            pltpu.VMEM((PW, PW), F32),
            DMA(()), DMA(()), DMA((2,)), DMA((2,)), DMA((15,)), DMA((15,)), DMA((7,)), DMA((4,)),
            DMA((15,)), DMA((15,)), DMA((16,)), DMA((16,)),
            DMA((30,)), DMA((32,)), DMA((32,)), DMA((32,)), DMA((32,)),
        ],
        compiler_params=pltpu.CompilerParams(
            collective_id=0, has_side_effects=True, vmem_limit_bytes=60 * MIB),
        name="front",
    )(border.reshape(2, 2, TB, TB), masked, barrier)


PER_STEP = 4


def schur_kernel(touched_ref, list_ref, count_ref, *refs):
    g_refs, h_refs = refs[:PER_STEP], refs[PER_STEP:2 * PER_STEP]
    bar_ref, out_ref, prod_ref = refs[2 * PER_STEP:]
    p, q = lax.axis_index("scen"), lax.axis_index("col")
    k = lax.rem(p, 8)
    step = pl.program_id(0)
    diagonal = k == q

    @pl.when(step == 0)
    def _():
        out_ref[...] = jnp.zeros_like(out_ref)

        @pl.when(diagonal)
        def _():
            eye = lax.broadcasted_iota(jnp.int32, (TB, TB), 0) == lax.broadcasted_iota(
                jnp.int32, (TB, TB), 1
            )
            for a in range(4):
                col = lane((2 * a + p // 8) * TB)
                row = bar_ref[pl.ds(a * 16 + p, 1), :]
                out_ref[a * TB:(a + 1) * TB, pl.ds(col, TB)] = jnp.where(eye, row, 0.0)

    @pl.when(step * PER_STEP < count_ref[0])
    def _():
        for i in range(PER_STEP):
            right = g_refs[i][0]
            left = jnp.where(diagonal, right, h_refs[i][0])
            prod_ref[i] = lax.dot_general(left, right, TN, preferred_element_type=F32)

        for i in range(PER_STEP):
            @pl.when(step * PER_STEP + i < count_ref[0])
            def _():
                s = list_ref[step * PER_STEP + i]
                row = pl.multiple_of((touched_ref[s * KT + k] // 16) * TB, TB)
                col = lane((touched_ref[s * KT + q] // 8) * TB)
                out_ref[pl.ds(row, TB), pl.ds(col, TB)] += prod_ref[i]


def assemble(touched, gathered, rows, barrier):
    p = lax.axis_index("scen")
    index = jnp.arange(SCEN, dtype=jnp.int32)
    mine = lax.dynamic_index_in_dim(touched, lax.rem(p, 8), 1, keepdims=False) % 16 == p
    place_of = jnp.sum(jnp.where(mine[None, :] & (index[None, :] < index[:, None]), 1, 0), axis=1)
    listed = jnp.sum(
        jnp.where(mine[None, :] & (place_of[None, :] == index[:, None]), index[None, :], 0), axis=1)
    count = jnp.sum(mine.astype(jnp.int32)).reshape(1)
    blocks = [
        pl.BlockSpec((1, TB, TB), lambda i, t, l, c, j=j: (l[i * PER_STEP + j], 0, 0))
        for j in range(PER_STEP)
    ]
    return pl.pallas_call(
        schur_kernel,
        out_shape=jax.ShapeDtypeStruct((1024, 2048), F32),
        grid_spec=pltpu.PrefetchScalarGridSpec(
            num_scalar_prefetch=3,
            grid=(SCEN // PER_STEP,),
            in_specs=blocks + blocks + [pl.BlockSpec((N // TB, TB), lambda i, t, l, c: (0, 0))],
            out_specs=pl.BlockSpec((1024, 2048), lambda i, t, l, c: (0, 0)),
            scratch_shapes=[pltpu.VMEM((PER_STEP, TB, TB), F32)],
        ),
        compiler_params=pltpu.CompilerParams(vmem_limit_bytes=60 * MIB),
        name="assemble",
    )(touched.reshape(-1), listed, count, *[gathered.reshape(SCEN, TB, TB)] * PER_STEP,
      *[rows.reshape(SCEN, TB, TB)] * PER_STEP, barrier)


def pivot_pair(a, b, d):
    q0 = lax.rsqrt(a)
    q1 = lax.rsqrt(a * (a * d - b * b))
    inv = q1 * q1 * a
    return q0, q1, d * inv, b * inv, a * inv


def pivot_four(w):
    (w00,), (w10, w11), (w20, w21, w22), (w30, w31, w32, w33) = w
    q0, q1, ci, bi, ai = pivot_pair(w00, w10, w11)
    e02, e12 = ci * w20 - bi * w21, ai * w21 - bi * w20
    e03, e13 = ci * w30 - bi * w31, ai * w31 - bi * w30
    v22 = w22 - w20 * e02 - w21 * e12
    v32 = w32 - w30 * e02 - w31 * e12
    v33 = w33 - w30 * e03 - w31 * e13
    q2, q3, cj, bj, aj = pivot_pair(v22, v32, v33)

    def solve(r0, r1, r2, r3):
        z0, z1 = ci * r0 - bi * r1, ai * r1 - bi * r0
        s2, s3 = r2 - w20 * z0 - w21 * z1, r3 - w30 * z0 - w31 * z1
        z2, z3 = cj * s2 - bj * s3, aj * s3 - bj * s2
        return z0 - e02 * z2 - e03 * z3, z1 - e12 * z2 - e13 * z3, z2, z3, s2, s3

    def half(r0, r1, s2, s3):
        return [r0 * q0, (w00 * r1 - w10 * r0) * q1, s2 * q2, (v22 * s3 - v32 * s2) * q3]

    return solve, half


def splat(row, at):
    return jnp.broadcast_to(row[:, at:at + 1], (1, NB))


HB = NB // 2


def small_inverse(a):
    eye = (
        lax.broadcasted_iota(jnp.int32, (HB, HB), 0)
        == lax.broadcasted_iota(jnp.int32, (HB, HB), 1)
    ).astype(F32)
    t = jnp.concatenate([a, eye], axis=1)
    top, rows, w = 0, [], None
    for o in range(0, HB, 4):
        if 8 * (o // 8) > top:
            t, top = t[8 * (o // 8) - top:], 8 * (o // 8)
        k, height = o - top, t.shape[0]
        c = [jnp.broadcast_to(t[:, o + i:o + i + 1], (height, NB)) for i in range(4)]
        r = [t[k + i:k + i + 1, :] for i in range(4)]
        if w is None:
            w = [[c[v][k + u:k + u + 1, :] for v in range(u + 1)] for u in range(4)]
        solve, half = pivot_four(w)
        last = o + 4 == HB
        if not last:
            after = [t[k + 4 + i:k + 5 + i, :] for i in range(4)]
            g = [[splat(r[i], o + 4 + u) for u in range(4)] for i in range(4)]
            z = [solve(*[g[i][v] for i in range(4)]) for v in range(4)]
            w = [[splat(after[u], o + 4 + v)
                  - (g[0][u] * z[v][0] + g[1][u] * z[v][1])
                  - (g[2][u] * z[v][2] + g[3][u] * z[v][3]) for v in range(u + 1)]
                 for u in range(4)]
        z0, z1, z2, z3, s2, s3 = solve(*r)
        rows += half(r[0], r[1], s2, s3)
        if not last:
            t = t - (c[0] * z0 + c[1] * z1) - (c[2] * z2 + c[3] * z3)
    return jnp.concatenate(rows, 0)[:, HB:NB]


def wide(a, b, dims=(((1,), (0,)), ((), ()))):
    return lax.dot_general(a, b, dims, precision=HIGHEST, preferred_element_type=F32)


def thirds(v):
    a = v.astype(BF16)
    rest = v - a.astype(F32)
    b = rest.astype(BF16)
    return a, b, (rest - b.astype(F32)).astype(BF16)


def left_parts(v):
    a, b, c = thirds(v)
    return jnp.concatenate([a, a, b, b, a, c], axis=1)


def right_parts(v, axis):
    a, b, c = thirds(v)
    return jnp.concatenate([a, b, a, b, c, a], axis=axis)


def invert_factor(a):
    x1 = small_inverse(a[:HB, :HB])
    l = wide(a[HB:, :HB], x1, NT)
    x2 = small_inverse(a[HB:, HB:] - wide(l, l, NT))
    x21 = -wide(wide(x2, l), x1)
    return jnp.concatenate([
        jnp.concatenate([x1, jnp.zeros((HB, HB), F32)], 1),
        jnp.concatenate([x21, x2], 1)], 0)


def panel_kernel(s_ref, w_hbm, pc_ref, pr_ref, pan_ref, w_ref, raw_ref, pf_ref, pb_ref,
                 loc, asend, arecv, wsend, wrecv, ssem, rsem,
                 zsend, zrecv, csend, crecv, fsend, frecv):
    p, q, x, y, z, c = place()
    here, partner = (p, q), dev(x, y, z, 1 - c)
    twin = (8 * (p // 8) + q, lax.rem(p, 8))
    alone = lax.rem(p, 8) == q
    bar = pltpu.get_barrier_semaphore()
    for d in plane_peers() + [(p, lax.rem(q + i, 8)) for i in range(1, 8)]:
        pl.semaphore_signal(bar, inc=1, device_id=d, device_id_type=MESH)

    @pl.when(alone)
    def _():
        pl.semaphore_wait(bar, 11)

    @pl.when(jnp.logical_not(alone))
    def _():
        pl.semaphore_signal(bar, inc=1, device_id=twin, device_id_type=MESH)
        pl.semaphore_wait(bar, 12)

    holds = q < 4
    mine = lane(lax.rem(q, 4) * TB)

    def rows_to(i):
        to = lax.rem(q + i, 8)
        return remote(s_ref.at[pl.ds(16 * to, 16), :, pl.ds(0, TB)],
                      raw_ref.at[:, :, pl.ds(mine, TB)],
                      asend.at[i - 1], arecv.at[lax.rem(q, 4)], (p, to))

    own_rows = pltpu.make_async_copy(
        s_ref.at[pl.ds(16 * q, 16), :, pl.ds(0, TB)], raw_ref.at[:, :, pl.ds(mine, TB)], loc.at[0])
    inverse = pltpu.make_async_copy(w_hbm, w_ref, loc.at[1])

    @pl.when(holds)
    def _():
        for i in (2, 3, 4, 5, 6, 1, 7):
            rows_to(i).start()
        own_rows.start()

    inverse.start()
    for m in range(4):
        @pl.when(q == m)
        def _():
            own_rows.wait()

        @pl.when(q != m)
        def _():
            t = raw_ref.at[:, :, pl.ds(m * TB, TB)]
            remote(t, t, asend.at[0], arecv.at[m], here).wait_recv()

    inverse.wait()
    for n in range(PW // NB):
        lo, hi = NB * n, NB * (n + 1)
        v = jnp.dot(raw_ref[:, :, 0:hi].reshape(NB, hi), w_ref[0:hi, lo:hi],
                    precision=HIGHEST, preferred_element_type=F32)
        pf_ref[:, :, lo:hi] = v.reshape(16, 8, NB)
        pb_ref[:, :, lo:hi] = v.astype(BF16).reshape(4, 32, NB)

    def to_twin():
        return remote(pb_ref, pc_ref.at[twin[0]], wsend, wrecv, twin)

    keep_cols = pltpu.make_async_copy(pb_ref, pc_ref.at[p], loc.at[2])
    keep_rows = pltpu.make_async_copy(pb_ref, pr_ref.at[q], loc.at[3])

    @pl.when(alone)
    def _():
        keep_cols.start()

    @pl.when(jnp.logical_not(alone))
    def _():
        to_twin().start()

    keep_rows.start()

    def over(i):
        return remote(pb_ref, pr_ref.at[q], zsend.at[i - 1], zrecv.at[i - 1],
                      dev(x, y, rem4(z + i), c))

    def across(i):
        src = pb_ref if i == 0 else pr_ref.at[2 * rem4(z - i) + c]
        return remote(src, pr_ref.at[2 * rem4(z - i) + c], csend.at[i], crecv.at[i], partner)

    def block(m):
        return remote(pf_ref.at[:, :, pl.ds(m * TB, TB)], pan_ref.at[q],
                      fsend.at[m], frecv.at[q], (p, m))

    def block_here(m):
        return pltpu.make_async_copy(
            pf_ref.at[:, :, pl.ds(m * TB, TB)], pan_ref.at[q], loc.at[4])

    plane = Plane(
        4, lambda j: pc_ref.at[p, j], lambda s: pc_ref.at[s // 4, lax.rem(s, 4)], ssem, rsem)

    @pl.when(alone)
    def _():
        keep_cols.wait()

    @pl.when(jnp.logical_not(alone))
    def _():
        remote(pb_ref, pc_ref.at[p], wsend, wrecv, twin).wait_recv()

    for n in range(len(COMBOS)):
        plane.event(*COMBOS[n])
        if n == 0:
            for i in (1, 3, 2):
                over(i).start()
            across(0).start()
            for m in range(4):
                @pl.when(q != m)
                def _():
                    block(m).start()

                @pl.when(q == m)
                def _():
                    block_here(m).start()
        if n in (4, 6, 8):
            i = {4: 1, 6: 3, 8: 2}[n]
            t = pr_ref.at[2 * rem4(z - i) + c]
            remote(t, t, zsend.at[0], zrecv.at[i - 1], here).wait_recv()
            across(i).start()
    plane.drain()
    keep_rows.wait()
    for i in (1, 2, 3):
        over(i).wait_send()
    for i in range(4):
        across(i).wait_send()
        t = pr_ref.at[2 * rem4(z - i) + 1 - c]
        remote(t, t, csend.at[0], crecv.at[i], here).wait_recv()
    for m in range(4):
        @pl.when(q != m)
        def _():
            block(m).wait_send()

        @pl.when(q == m)
        def _():
            block_here(m).wait()
            for i in range(1, 8):
                t = pan_ref.at[lax.rem(q + i, 8)]
                remote(t, t, fsend.at[0], frecv.at[lax.rem(q + i, 8)], here).wait_recv()

    @pl.when(jnp.logical_not(alone))
    def _():
        to_twin().wait_send()

    @pl.when(holds)
    def _():
        for i in range(1, 8):
            rows_to(i).wait_send()


def solve_panel(schur, inverse):
    hbm = pl.BlockSpec(memory_space=pl.ANY)
    return pl.pallas_call(
        panel_kernel,
        out_shape=(
            jax.ShapeDtypeStruct((16, 4, 32, PW), BF16),
            jax.ShapeDtypeStruct((8, 4, 32, PW), BF16),
            jax.ShapeDtypeStruct((8, 16, 8, TB), F32),
        ),
        in_specs=[hbm, hbm],
        out_specs=(hbm, hbm, hbm),
        scratch_shapes=[
            pltpu.VMEM((PW, PW), F32), pltpu.VMEM((16, 8, PW), F32),
            pltpu.VMEM((16, 8, PW), F32), pltpu.VMEM((4, 32, PW), BF16),
            DMA((5,)), DMA((7,)), DMA((4,)), DMA(()), DMA(()), DMA((60,)), DMA((64,)),
            DMA((3,)), DMA((3,)), DMA((4,)), DMA((4,)), DMA((4,)), DMA((8,)),
        ],
        compiler_params=pltpu.CompilerParams(
            collective_id=1, has_side_effects=True, vmem_limit_bytes=60 * MIB),
        name="solve_panel",
    )(schur.reshape(128, 8, 2048), inverse)


STRIP = 256


def update_kernel(s_ref, pr_ref, pc_ref, pan_ref, out_ref):
    p, q = lax.axis_index("scen"), lax.axis_index("col")
    a = pl.program_id(0) // (TB // STRIP)
    low = jnp.logical_or(a > 0, p >= 4)
    panel = q < 4
    for b in range(8):
        cols = slice(b * TB, (b + 1) * TB)
        first = (b % 2) * 1024 + (b // 2) * TB

        def lowered():
            out_ref[:, cols] = s_ref[:, cols] - lax.dot_general(
                pr_ref[...], pc_ref[first:first + TB, :], NT, preferred_element_type=F32)

        def kept():
            out_ref[:, cols] = s_ref[:, cols]

        def solved():
            out_ref[:, cols] = pan_ref[...]

        if b == 0:
            pl.when(panel)(solved)
            pl.when(jnp.logical_and(jnp.logical_not(panel), low))(lowered)
            pl.when(jnp.logical_and(jnp.logical_not(panel), jnp.logical_not(low)))(kept)
        else:
            pl.when(low)(lowered)
            pl.when(jnp.logical_not(low))(kept)


def update(schur, rows, cols, panel):
    strip = pl.BlockSpec((STRIP, 2048), lambda i: (i, 0))
    return pl.pallas_call(
        update_kernel,
        out_shape=jax.ShapeDtypeStruct((1024, 2048), F32),
        grid=(1024 // STRIP,),
        in_specs=[
            strip,
            pl.BlockSpec((STRIP, PW), lambda i: (i, 0)),
            pl.BlockSpec((2048, PW), lambda i: (0, 0)),
            pl.BlockSpec((STRIP, TB), lambda i: (i, 0)),
        ],
        out_specs=strip,
        compiler_params=pltpu.CompilerParams(vmem_limit_bytes=60 * MIB),
        name="update",
    )(schur, rows.reshape(1024, PW), cols.reshape(2048, PW), panel.reshape(1024, TB))


def per_device(border, touched, barrier):
    p, q = lax.axis_index("scen"), lax.axis_index("col")
    mine = lax.dynamic_slice(touched, (4 * p, q), (4, 1))
    masked = jnp.where((mine == q)[:, :, None], border, jnp.zeros_like(border))
    barrier = barrier.reshape(N // TB, TB)
    gathered, rows, inverse = front(border, masked, barrier)
    schur = assemble(touched, gathered, rows, barrier)
    panel_cols, panel_rows, panel = solve_panel(schur, inverse)
    return update(schur, panel_rows, panel_cols, panel)


def solution(mesh):
    in_specs = (P("scen", None, "col"), P(), P())
    out_specs = P("scen", "col")
    return jax.shard_map(
        per_device, mesh=mesh, in_specs=in_specs, out_specs=out_specs, check_vma=False
    )
```
